128 devices in a mesh: attn: 4 (over x), dev: 32 (over z, y, core).
Axes of the slice: x: 4, y: 4, z: 4, core: 2. Of those that a mesh axis runs over, the one named last changes fastest.
Arguments:
- queries: bfloat16 [2048, 8192], P(('attn', 'dev')), may hold values from -6 to 6
- new_keys: bfloat16 [2048, 512], P(('attn', 'dev')), may hold values from -6 to 6
- new_values: bfloat16 [2048, 512], P(('attn', 'dev')), may hold values from -6 to 6
- key_pages: bfloat16 [8192, 16, 512], P(('attn', 'dev')), may hold values from -6 to 6
- value_pages: bfloat16 [8192, 16, 512], P(('attn', 'dev')), may hold values from -6 to 6
- block_tables: int32 [2048, 4], P(('attn', 'dev')), may hold values from 0 to 63, as said below
- context_lengths: int32 [2048], P(('attn', 'dev')), may hold values from 1 to 64, as said below
- out_weight: bfloat16 [8192, 4096], P('dev'), may hold values from -0.0625 to 0.0625
- residual: bfloat16 [2048, 4096], P(('attn', 'dev')), may hold values from -6 to 6
- norm_gain: float32 [4096], replicated, may hold values from 0.5 to 1.5
- router_weight: bfloat16 [4096, 128], replicated, may hold values from -0.09375 to 0.09375
- routes: int32 [2048, 8], P(('attn', 'dev')), may hold values from 0 to 127, all different within a row; in each aligned block of 16 rows (0 to 15, 16 to 31, ...) at most 2 rows name the same one
- expert_gate: bfloat16 [128, 4096, 768], P(('attn', 'dev')), may hold values from -0.09375 to 0.09375
- expert_up: bfloat16 [128, 4096, 768], P(('attn', 'dev')), may hold values from -0.09375 to 0.09375
- expert_down: bfloat16 [128, 768, 4096], P(('attn', 'dev')), may hold values from -0.21875 to 0.21875
Outputs:
- layer_output: bfloat16 [2048, 4096], P(('attn', 'dev'))
The draws below stay inside these ranges and needn't reach their ends.
Inputs may be any that keep to these rules, and one draw needn't show every extreme that they name: `block_tables`: on the rows of one device (16 requests in order) the entries are a permutation of 0 to 63, that device's pages in order. `context_lengths`: the rows of every device hold a request of exactly 64 cached tokens. `routes`: the 8 entries of a row differ; within the rows of one device no expert is named by more than 2 rows.
All inputs are finite; a program needn't handle non-finite values.
Results may differ from the reference program's by a relative error of at most 0.02.
Values may be sent and summed in bfloat16 or wider, within the bound.
No kernel may reach another device: no remote copies, remote signals or barrier semaphores. Data moves between devices by JAX's collectives and lax.ppermute only.
A program may use at most 128 MiB of HBM per device.

```python
import math
import jax
import jax.numpy as jnp
import numpy as np
from jax import lax

D = 4096
HEADS = 64
KVH = 4
HD = 128
TOP = 8
FFE = 768
TOK_DEV = 16
PAGE = 16
MAXCTX = 64
EXPERTS = 128
PAGES_REQ = 4
PAGES_DEV = 64
TOKENS = 2048
POOL = 8192
CAP = 2
N_DEV = 32
DEVICES = 128


def draw_queries(key, part):
    key = jax.random.fold_in(key, 101)
    values = jnp.clip(jax.random.normal(key, (TOKENS, HEADS, HD), jnp.float32), -6.0, 6.0)
    return values.reshape(TOKENS, HEADS * HD).astype(jnp.bfloat16)


def draw_key_pages(key, part):
    key = jax.random.fold_in(key, 202)
    values = jnp.clip(jax.random.normal(key, (POOL, PAGE, KVH, HD), jnp.float32), -6.0, 6.0)
    return values.reshape(POOL, PAGE, KVH * HD).astype(jnp.bfloat16)


def draw_block_tables(key, part):
    key = jax.random.fold_in(key, 303)
    device_keys = jax.random.split(key, DEVICES)

    def one_device(device_key):
        return jax.random.permutation(device_key, PAGES_DEV)
    orders = jax.vmap(one_device)(device_keys)
    return orders.reshape(TOKENS, PAGES_REQ).astype(jnp.int32)


def draw_context_lengths(key, part):
    key = jax.random.fold_in(key, 404)
    first_key, second_key = jax.random.split(key)
    lengths = jax.random.randint(first_key, (DEVICES, TOK_DEV), 1, MAXCTX + 1)
    longest_at = jax.random.randint(second_key, (DEVICES,), 0, TOK_DEV)
    lengths = jnp.where(jnp.arange(TOK_DEV, dtype=jnp.int32)[None, :] == longest_at[:, None], MAXCTX, lengths)
    return lengths.reshape(TOKENS).astype(jnp.int32)


def block_scale(stream_key, shape, shards, low, largest):
    level = 1.0
    for axis_at, shards_of in shards:
        steps = jax.random.uniform(jax.random.fold_in(jax.random.fold_in(stream_key, 6), axis_at), (shards_of,), jnp.float32, low / len(shards), largest / len(shards))
        level = level * jnp.repeat(jnp.exp(steps), shape[axis_at] // shards_of).reshape((-1,) + (1,) * (len(shape) - 1 - axis_at))
    return level


def assign_block(key, own, number, rows, number_of, top, bound, slope):
    ranking = jax.random.permutation(key, number_of)
    crowded, usual = shares(number_of, rows * top, bound, slope, True), shares(number_of, rows * top, bound, slope, False)
    places = jnp.arange(number_of)

    def named(sizes, turn):
        used = int((sizes > 0).sum())
        fixed = max(1, used // 4)
        passed = fixed + (places - fixed + turn * (used - fixed)) % max(1, number_of - fixed)
        return jnp.zeros((number_of,), jnp.int32).at[ranking[jnp.where(places < fixed, places, passed)]].set(jnp.asarray(sizes, jnp.int32))

    sizes = jnp.where(number % 4 == 0, named(crowded, number // 4), named(usual, number - number // 4 - 1))
    mixed = jax.random.permutation(jax.random.fold_in(own, 3), number_of)
    source_of, sink = mixed[0:number_of // 2 * 2:2], mixed[1:number_of // 2 * 2:2]
    slack = jnp.minimum(sizes[source_of] - 1, bound - sizes[sink]) // 2
    slack = jnp.where((source_of == ranking[0]) | (sink == ranking[0]) | (sizes[sink] == 0), 0, jnp.maximum(slack, 0))
    passed = jax.random.randint(jax.random.fold_in(own, 4), (number_of // 2,), 0, 1 << 20) % (slack + 1)
    sizes = sizes.at[source_of].add(-passed).at[sink].add(passed)
    labels = jnp.searchsorted(jnp.cumsum(sizes), jnp.arange(rows * top), side="right").astype(jnp.int32)
    grid = labels.reshape(top, rows).T
    grid = grid[jax.random.permutation(jax.random.fold_in(own, 1), rows)]
    turn = jax.random.randint(jax.random.fold_in(own, 2), (rows, 1), 0, top)
    return jnp.take_along_axis(grid, (jnp.arange(top)[None, :] + turn) % top, axis=1)


def shares(amount, total, most, skew, full):
    loads = [(1 << 20) // math.isqrt(grade ** skew) + 1 for grade in range(1, amount + 1)]
    largest = most if full else min(most, max(-(-total // amount), total * loads[0] // sum(loads)))
    least = 1 if total - largest >= amount - 1 else 0
    holding, rest = [largest] + [least] * (amount - 1), total - largest - least * (amount - 1)
    while rest > 0:
        free = [i for i in range(1, amount) if holding[i] < largest] or [i for i in range(1, amount) if holding[i] < most]
        mass, remaining = sum([loads[i] for i in free]), rest
        for i in free:
            more = min(most - holding[i], max(1, remaining * loads[i] // mass), rest)
            holding[i] = holding[i] + more
            rest = rest - more
    return np.array(holding)


def gaussian(key, extent, scale, bound, shards=(), kind=jnp.bfloat16):
    level = block_scale(key, extent, shards, -0.22, 0.18) if shards else 1.0
    values = jax.random.normal(key, extent, jnp.float32) * scale * level
    return jnp.minimum(jnp.maximum(values, -bound), bound).astype(kind)


def setup_inputs(seed: int = 0) -> dict:
    streams_of = jax.random.split(jax.random.key(seed), 16)
    queries = draw_queries(jax.random.fold_in(streams_of[15], 71), 0)
    new_keys = gaussian(streams_of[1], (TOKENS, KVH * HD), 1.0, 6.0, ((0, 128),))
    new_values = gaussian(streams_of[2], (TOKENS, KVH * HD), 1.0, 6.0, ((0, 128),))
    key_pages = draw_key_pages(jax.random.fold_in(streams_of[15], 71), 0)
    value_pages = gaussian(streams_of[4], (POOL, PAGE, KVH * HD), 1.0, 6.0, ((0, 128),))
    block_tables = draw_block_tables(jax.random.fold_in(streams_of[15], 71), 0)
    context_lengths = draw_context_lengths(jax.random.fold_in(streams_of[15], 71), 0)
    out_weight = gaussian(streams_of[7], (HEADS * HD, D), (HEADS * HD) ** -0.5, 0.0625, ((0, 32),))
    residual = gaussian(streams_of[8], (TOKENS, D), 1.0, 6.0, ((0, 128),))
    norm_gain = jnp.clip(1.0 + 0.1 * jax.random.normal(streams_of[9], (D,), jnp.float32), 0.5, 1.5)
    router_weight = gaussian(streams_of[10], (D, EXPERTS), D ** -0.5, 0.09375)
    routes_keys = jax.random.split(jax.random.fold_in(streams_of[11], 1), TOKENS // TOK_DEV)
    routes_turns = jax.random.permutation(jax.random.fold_in(streams_of[11], 3), TOKENS // TOK_DEV)
    routes = jax.vmap(lambda own, number: assign_block(jax.random.fold_in(streams_of[11], 2), own, number, TOK_DEV, EXPERTS, TOP, CAP, 1))(routes_keys, routes_turns).reshape((TOKENS, TOP))
    expert_gate = gaussian(streams_of[12], (EXPERTS, D, FFE), D ** -0.5, 0.09375, ((0, 128),))
    expert_up = gaussian(streams_of[13], (EXPERTS, D, FFE), D ** -0.5, 0.09375, ((0, 128),))
    expert_down = gaussian(streams_of[14], (EXPERTS, FFE, D), FFE ** -0.5, 0.21875, ((0, 128),))
    return {"queries": queries, "new_keys": new_keys, "new_values": new_values, "key_pages": key_pages, "value_pages": value_pages, "block_tables": block_tables, "context_lengths": context_lengths, "out_weight": out_weight, "residual": residual, "norm_gain": norm_gain, "router_weight": router_weight, "routes": routes, "expert_gate": expert_gate, "expert_up": expert_up, "expert_down": expert_down}


EPSILON = 1e-06
HIGHEST = lax.Precision.HIGHEST

def attend(queries, new_keys, new_values, key_pool, value_pool, tables, lengths):
    count_rows = queries.shape[0]
    group_size = HEADS // KVH
    query_heads = queries.astype(jnp.float32).reshape(count_rows, KVH, group_size, HD)
    cached_keys = key_pool[tables].astype(jnp.float32).reshape(count_rows, MAXCTX, KVH, HD)
    cached_values = value_pool[tables].astype(jnp.float32).reshape(count_rows, MAXCTX, KVH, HD)
    own_key = new_keys.astype(jnp.float32).reshape(count_rows, KVH, HD)
    own_value = new_values.astype(jnp.float32).reshape(count_rows, KVH, 1, HD)
    scale_factor = 1.0 / math.sqrt(HD)
    scores = jnp.einsum('rkgh,rskh->rkgs', query_heads, cached_keys, precision=HIGHEST) * scale_factor
    own_score = jnp.einsum('rkgh,rkh->rkg', query_heads, own_key, precision=HIGHEST) * scale_factor
    live_mask = jnp.arange(MAXCTX, dtype=jnp.int32)[None, :] < lengths[:, None]
    scores = jnp.where(live_mask[:, None, None, :], scores, -jnp.inf)
    top_score = jnp.maximum(lax.optimization_barrier(jnp.max(scores, axis=-1)), own_score)
    weights = jnp.exp(scores - top_score[..., None])
    own_weight = jnp.exp(own_score - top_score)
    total_mass = lax.optimization_barrier(jnp.sum(weights, axis=-1)) + own_weight
    weights = lax.optimization_barrier((weights / total_mass[..., None]).astype(jnp.bfloat16))
    own_weight = lax.optimization_barrier((own_weight / total_mass).astype(jnp.bfloat16))
    blended = jnp.einsum('rkgs,rskh->rkgh', weights.astype(jnp.float32), cached_values, precision=HIGHEST)
    blended = blended + own_weight.astype(jnp.float32)[..., None] * own_value
    return blended.reshape(count_rows, HEADS * HD).astype(jnp.bfloat16)

def rms_norm(hidden_state, norm_gain):
    mean_square = lax.optimization_barrier(jnp.mean(hidden_state * hidden_state, axis=-1, keepdims=True))
    return (hidden_state * lax.rsqrt(mean_square + EPSILON) * norm_gain).astype(jnp.bfloat16)

def route_gates(logits, routes):
    matches = routes[:, :, None] == jnp.arange(logits.shape[1], dtype=jnp.int32)[None, None, :]
    chosen = lax.optimization_barrier(jnp.sum(jnp.where(matches, logits[:, None, :], 0.0), axis=-1))
    raised = jnp.exp(chosen)
    return raised / lax.optimization_barrier(jnp.sum(raised, axis=1, keepdims=True))

def slot_index(flat_routes, experts, capacity):
    onehot = (flat_routes[:, None] == jnp.arange(experts, dtype=jnp.int32)[None, :]).astype(jnp.int32)
    earlier = jnp.cumsum(onehot, axis=0) - onehot
    rank_within = lax.optimization_barrier(jnp.sum(earlier * onehot, axis=1))
    return flat_routes * capacity + rank_within

def reference(queries, new_keys, new_values, key_pages, value_pages, block_tables, context_lengths, out_weight, residual, norm_gain, router_weight, routes, expert_gate, expert_up, expert_down):

    def per_device(array):
        return array.reshape((DEVICES, TOK_DEV) + array.shape[1:])

    def attend_block(packed):
        return attend(*packed)
    attended = lax.map(attend_block, (per_device(queries), per_device(new_keys), per_device(new_values), key_pages.reshape(DEVICES, PAGES_DEV, PAGE, KVH * HD), value_pages.reshape(DEVICES, PAGES_DEV, PAGE, KVH * HD), per_device(block_tables), per_device(context_lengths)))
    attended = attended.reshape(TOKENS, HEADS * HD)
    width_part = HEADS * HD // N_DEV

    def add_part(running, block_index):
        offset = (block_index * width_part).astype(jnp.int32)
        columns = lax.dynamic_slice_in_dim(attended, offset, width_part, 1).astype(jnp.float32)
        weight_rows = lax.dynamic_slice_in_dim(out_weight, offset, width_part, 0).astype(jnp.float32)
        partial_term = jnp.dot(columns, weight_rows, precision=HIGHEST).astype(jnp.bfloat16)
        partial_term = lax.optimization_barrier(partial_term)
        return (running + partial_term.astype(jnp.float32), None)
    projected, unused = lax.scan(add_part, jnp.zeros((TOKENS, D), jnp.float32), jnp.arange(N_DEV, dtype=jnp.int32))
    hidden_state = residual.astype(jnp.float32) + projected
    normed = rms_norm(hidden_state, norm_gain)
    logits = jnp.dot(normed.astype(jnp.float32), router_weight.astype(jnp.float32), precision=HIGHEST)
    gate_values = route_gates(logits, routes)

    def slots_of_device(flat_routes):
        return slot_index(flat_routes, EXPERTS, CAP)
    slot_of = jax.vmap(slots_of_device)(routes.reshape(DEVICES, TOK_DEV * TOP))
    token_ids = jnp.broadcast_to(jnp.arange(TOK_DEV, dtype=jnp.int32)[:, None], (TOK_DEV, TOP)).reshape(-1)
    device_ids = jnp.arange(DEVICES, dtype=jnp.int32)[:, None]
    slot_token = jnp.full((DEVICES, EXPERTS * CAP), TOK_DEV, jnp.int32).at[device_ids, slot_of].set(token_ids[None, :])
    padded_rows = jnp.concatenate([normed.reshape(DEVICES, TOK_DEV, D), jnp.zeros((DEVICES, 1, D), jnp.bfloat16)], axis=1)

    def run_expert(packed):
        expert_index, w_gate, w_up, w_down = packed
        token_index = lax.dynamic_slice_in_dim(slot_token, (expert_index * CAP).astype(jnp.int32), CAP, 1)
        gathered = padded_rows[device_ids, token_index].reshape(DEVICES * CAP, D).astype(jnp.float32)
        gate_part = jnp.dot(gathered, w_gate.astype(jnp.float32), precision=HIGHEST)
        up_part = jnp.dot(gathered, w_up.astype(jnp.float32), precision=HIGHEST)
        expert_hidden = lax.optimization_barrier((jax.nn.silu(gate_part) * up_part).astype(jnp.bfloat16))
        output_rows = jnp.dot(expert_hidden.astype(jnp.float32), w_down.astype(jnp.float32), precision=HIGHEST)
        return output_rows.astype(jnp.bfloat16).reshape(DEVICES, CAP, D)
    expert_output = lax.map(run_expert, (jnp.arange(EXPERTS, dtype=jnp.int32), expert_gate, expert_up, expert_down))

    def combine_block(packed):
        experts_here, ranks_here, gates_here, device_index = packed
        chosen_rows = expert_output[experts_here, device_index, ranks_here].astype(jnp.float32)
        return lax.optimization_barrier(jnp.sum(chosen_rows * gates_here[:, :, None], axis=1))
    expert_sum = lax.map(combine_block, (routes.reshape(DEVICES, TOK_DEV, TOP), (slot_of % CAP).reshape(DEVICES, TOK_DEV, TOP), gate_values.reshape(DEVICES, TOK_DEV, TOP), jnp.arange(DEVICES, dtype=jnp.int32)))
    return (hidden_state + expert_sum.reshape(TOKENS, D)).astype(jnp.bfloat16)
```

```python
import math

import jax
import jax.numpy as jnp
from jax import lax
from jax.sharding import PartitionSpec as P

HEADS = 64
KVH = 4
HD = 128
MAXCTX = 64
EPSILON = 1e-06
BLOCK = 512


def attend(queries, new_keys, new_values, key_pool, value_pool, tables, lengths):
    count_rows = queries.shape[0]
    group_size = HEADS // KVH
    query_heads = queries.reshape(count_rows, KVH, group_size, HD)
    cached_keys = key_pool[tables].reshape(count_rows, MAXCTX, KVH, HD)
    cached_values = value_pool[tables].reshape(count_rows, MAXCTX, KVH, HD)
    own_key = new_keys.reshape(count_rows, KVH, HD)
    own_value = new_values.reshape(count_rows, KVH, 1, HD).astype(jnp.float32)
    scale_factor = 1.0 / math.sqrt(HD)
    scores = (
        jnp.einsum("rkgh,rskh->rkgs", query_heads, cached_keys, preferred_element_type=jnp.float32)
        * scale_factor
    )
    own_score = (
        jnp.einsum("rkgh,rkh->rkg", query_heads, own_key, preferred_element_type=jnp.float32)
        * scale_factor
    )
    live_mask = jnp.arange(MAXCTX, dtype=jnp.int32)[None, :] < lengths[:, None]
    scores = jnp.where(live_mask[:, None, None, :], scores, -jnp.inf)
    top_score = jnp.maximum(jnp.max(scores, axis=-1), own_score)
    weights = jnp.exp(scores - top_score[..., None])
    own_weight = jnp.exp(own_score - top_score)
    total_mass = jnp.sum(weights, axis=-1) + own_weight
    weights = (weights / total_mass[..., None]).astype(jnp.bfloat16)
    own_weight = lax.optimization_barrier((own_weight / total_mass).astype(jnp.bfloat16))
    blended = jnp.einsum(
        "rkgs,rskh->rkgh", weights, cached_values, preferred_element_type=jnp.float32
    )
    blended = blended + own_weight.astype(jnp.float32)[..., None] * own_value
    return blended.reshape(count_rows, HEADS * HD).astype(jnp.bfloat16)


def route_gates(logits, routes):
    matches = routes[:, :, None] == jnp.arange(logits.shape[1], dtype=jnp.int32)[None, None, :]
    chosen = jnp.sum(jnp.where(matches, logits[:, None, :], 0.0), axis=-1)
    raised = jnp.exp(chosen)
    return raised / jnp.sum(raised, axis=1, keepdims=True)


def slot_index(flat_routes, experts, capacity):
    onehot = (flat_routes[:, None] == jnp.arange(experts, dtype=jnp.int32)[None, :]).astype(
        jnp.int32
    )
    earlier = jnp.cumsum(onehot, axis=0) - onehot
    rank_within = jnp.sum(earlier * onehot, axis=1)
    return flat_routes * capacity + rank_within


def shards(
    queries,
    new_keys,
    new_values,
    key_pages,
    value_pages,
    block_tables,
    context_lengths,
    out_weight,
    residual,
    norm_gain,
    router_weight,
    routes,
    expert_gate,
    expert_up,
    expert_down,
):
    rows = queries.shape[0]
    width = out_weight.shape[1]
    depth = out_weight.shape[0]
    peers = lax.axis_size("dev")
    chips = peers // 2
    core = lax.axis_index("dev") % 2
    same_core = [[2 * chip + side for chip in range(chips)] for side in range(2)]
    experts = router_weight.shape[1]
    capacity = 2
    blocks = width // BLOCK

    weight_beside = lax.ppermute(out_weight, "dev", [(i, i ^ 1) for i in range(peers)])
    attended = attend(
        queries, new_keys, new_values, key_pages, value_pages, block_tables, context_lengths
    )
    outgoing = attended.reshape(rows, chips, 2 * depth).transpose(1, 0, 2)
    regrouped = lax.all_to_all(
        outgoing, "dev", split_axis=0, concat_axis=0, axis_index_groups=same_core, tiled=True
    ).reshape(chips * rows, 2 * depth)
    first, second = regrouped[:, :depth], regrouped[:, depth:]
    mine = jnp.where(core == 0, first, second)
    beside = jnp.where(core == 0, second, first)
    partial = (
        jnp.dot(mine, out_weight, preferred_element_type=jnp.float32)
        + jnp.dot(beside, weight_beside, preferred_element_type=jnp.float32)
    ).astype(jnp.bfloat16)
    partials = lax.all_to_all(
        partial.reshape(chips, rows, width),
        "dev",
        split_axis=0,
        concat_axis=0,
        axis_index_groups=same_core,
        tiled=True,
    )
    hidden_state = residual.astype(jnp.float32) + jnp.sum(partials.astype(jnp.float32), axis=0)

    mean_square = jnp.mean(hidden_state * hidden_state, axis=-1, keepdims=True)
    normed = (hidden_state * lax.rsqrt(mean_square + EPSILON) * norm_gain).astype(jnp.bfloat16)
    logits = jnp.dot(normed, router_weight, preferred_element_type=jnp.float32)
    gate_values = route_gates(logits, routes)

    slot_of = slot_index(routes.reshape(-1), experts, capacity).reshape(rows, -1)
    line = jnp.arange(experts * blocks * capacity, dtype=jnp.int32)
    line_slot = line // (blocks * capacity) * capacity + line % capacity
    line_block = line // capacity % blocks
    cell = jnp.arange(blocks * rows, dtype=jnp.int32)
    same_block = line_block[:, None] == (cell // rows)[None, :]
    slot_of_cell = jnp.tile(slot_of, (blocks, 1))
    hit = (line_slot[:, None, None] == slot_of_cell[None, :, :]) & same_block[:, :, None]
    placing = jnp.any(hit, axis=2).astype(jnp.bfloat16)
    stacked = normed.reshape(rows, blocks, BLOCK).transpose(1, 0, 2).reshape(blocks * rows, BLOCK)
    sent = jnp.dot(placing, stacked, preferred_element_type=jnp.float32).astype(jnp.bfloat16)
    arrived = lax.all_to_all(
        sent.reshape(experts, blocks * capacity, BLOCK),
        ("attn", "dev"),
        split_axis=0,
        concat_axis=0,
        tiled=True,
    )
    flat_rows = (
        arrived.reshape(experts, blocks, capacity, BLOCK)
        .transpose(2, 0, 1, 3)
        .reshape(experts * capacity, width)
    )
    gate_part = jnp.dot(flat_rows, expert_gate[0], preferred_element_type=jnp.float32)
    up_part = jnp.dot(flat_rows, expert_up[0], preferred_element_type=jnp.float32)
    expert_hidden = (jax.nn.silu(gate_part) * up_part).astype(jnp.bfloat16)
    output_rows = jnp.dot(
        expert_hidden, expert_down[0], preferred_element_type=jnp.float32
    ).astype(jnp.bfloat16)
    back = (
        output_rows.reshape(capacity, experts, blocks, BLOCK)
        .transpose(1, 2, 0, 3)
        .reshape(experts, blocks * capacity, BLOCK)
    )
    returned = lax.all_to_all(
        back, ("attn", "dev"), split_axis=0, concat_axis=0, tiled=True
    ).reshape(experts * blocks * capacity, BLOCK)
    gate_of_cell = jnp.tile(gate_values, (blocks, 1))
    mixing = jnp.sum(jnp.where(hit, gate_of_cell[None, :, :], 0.0), axis=2).T
    high = mixing.astype(jnp.bfloat16)
    low = (mixing - high.astype(jnp.float32)).astype(jnp.bfloat16)
    mixed = jnp.dot(
        jnp.concatenate([high, low], axis=0), returned, preferred_element_type=jnp.float32
    )
    mixed = mixed[: blocks * rows] + mixed[blocks * rows :]
    expert_sum = mixed.reshape(blocks, rows, BLOCK).transpose(1, 0, 2).reshape(rows, width)
    return (hidden_state + expert_sum).astype(jnp.bfloat16)


def solution(mesh):
    in_specs = (
        P(("attn", "dev"), None),
        P(("attn", "dev"), None),
        P(("attn", "dev"), None),
        P(("attn", "dev"), None, None),
        P(("attn", "dev"), None, None),
        P(("attn", "dev"), None),
        P(("attn", "dev")),
        P("dev", None),
        P(("attn", "dev"), None),
        P(),
        P(),
        P(("attn", "dev"), None),
        P(("attn", "dev"), None, None),
        P(("attn", "dev"), None, None),
        P(("attn", "dev"), None, None),
    )
    out_specs = P(("attn", "dev"), None)
    return jax.shard_map(shards, mesh=mesh, in_specs=in_specs, out_specs=out_specs, check_vma=False)
```

```python
import functools
import math

import jax
import jax.numpy as jnp
from jax import lax
from jax.experimental import pallas as pl
from jax.experimental.pallas import tpu as pltpu
from jax.sharding import PartitionSpec as P

HEADS = 64
KVH = 4
HD = 128
GROUP = HEADS // KVH
MAXCTX = 64
PAGE = 16
EPSILON = 1e-06
BLOCK = 512
TOGETHER = 4
CONTRACT_LAST = (((1,), (1,)), ((), ()))
VMEM = pl.BlockSpec(memory_space=pltpu.VMEM)
SMEM = pl.BlockSpec(memory_space=pltpu.SMEM)


def attention_kernel(
    tables, lengths, q_ref, own_key, own_value, keys, values, out_ref, q_turned, out_turned
):
    rows = q_ref.shape[0]
    pages = MAXCTX // PAGE
    tall, wide = TOGETHER * GROUP, TOGETHER * MAXCTX
    scale = 1.0 / math.sqrt(HD)
    for head in range(HEADS):
        q_turned[head // GROUP, pl.ds(head % GROUP * rows, rows), :] = q_ref[
            :, head * HD : (head + 1) * HD
        ].astype(jnp.float32)
    row_request = lax.broadcasted_iota(jnp.int32, (tall, wide), 0) // GROUP
    column = lax.broadcasted_iota(jnp.int32, (tall, wide), 1)
    own_row = lax.broadcasted_iota(jnp.int32, (tall, rows), 0) // GROUP
    own_column = lax.broadcasted_iota(jnp.int32, (tall, rows), 1)
    for first in range(0, rows, TOGETHER):
        limit = jnp.zeros((tall, wide), jnp.int32)
        for i in range(TOGETHER):
            limit = jnp.where(row_request == i, lengths[first + i], limit)
        place = column - row_request * MAXCTX
        live = (place >= 0) & (place < limit)
        is_own = own_column == own_row + first
        page_ids = [tables[first + i, j] for i in range(TOGETHER) for j in range(pages)]
        for kv in range(KVH):
            lanes = slice(kv * HD, (kv + 1) * HD)
            q = jnp.concatenate(
                [
                    q_turned[kv, pl.ds(first + i, GROUP, stride=rows), :]
                    for i in range(TOGETHER)
                ],
                axis=0,
            ).astype(jnp.bfloat16)
            k = jnp.concatenate([keys[page, :, lanes] for page in page_ids], axis=0)
            v = jnp.concatenate([values[page, :, lanes] for page in page_ids], axis=0)
            scores = (
                lax.dot_general(q, k, CONTRACT_LAST, preferred_element_type=jnp.float32) * scale
            )
            own_score = (
                lax.dot_general(
                    q, own_key[:, lanes], CONTRACT_LAST, preferred_element_type=jnp.float32
                )
                * scale
            )
            scores = jnp.where(live, scores, -jnp.inf)
            own_score = jnp.where(is_own, own_score, -jnp.inf)
            top = jnp.maximum(
                jnp.max(scores, axis=1, keepdims=True), jnp.max(own_score, axis=1, keepdims=True)
            )
            weights = jnp.exp(scores - top)
            own_weight = jnp.exp(own_score - top)
            total = jnp.sum(weights, axis=1, keepdims=True) + jnp.sum(
                own_weight, axis=1, keepdims=True
            )
            share = 1.0 / total
            blended = jnp.dot(
                (weights * share).astype(jnp.bfloat16), v, preferred_element_type=jnp.float32
            ) + jnp.dot(
                (own_weight * share).astype(jnp.bfloat16),
                own_value[:, lanes],
                preferred_element_type=jnp.float32,
            )
            for i in range(TOGETHER):
                out_turned[kv, pl.ds(first + i, GROUP, stride=rows), :] = blended[
                    i * GROUP : (i + 1) * GROUP
                ]
    held = out_ref.shape[2] // HD
    for head in range(HEADS):
        out_ref[head // held, :, head % held * HD : (head % held + 1) * HD] = out_turned[
            head // GROUP, pl.ds(head % GROUP * rows, rows), :
        ].astype(jnp.bfloat16)


def attend(queries, new_keys, new_values, key_pool, value_pool, tables, lengths, chips):
    rows = queries.shape[0]
    return pl.pallas_call(
        attention_kernel,
        out_shape=jax.ShapeDtypeStruct((chips, rows, HEADS * HD // chips), jnp.bfloat16),
        in_specs=[SMEM, SMEM, VMEM, VMEM, VMEM, VMEM, VMEM],
        out_specs=VMEM,
        scratch_shapes=[
            pltpu.VMEM((KVH, GROUP * rows, HD), jnp.float32),
            pltpu.VMEM((KVH, GROUP * rows, HD), jnp.float32),
        ],
        compiler_params=pltpu.CompilerParams(vmem_limit_bytes=24 << 20),
        cost_estimate=pl.CostEstimate(
            flops=600_000_000, bytes_accessed=5_000_000, transcendentals=300_000
        ),
        name="attention",
    )(tables, lengths, queries, new_keys, new_values, key_pool, value_pool)


def projection_kernel(masks, spot, x_ref, mine_ref, beside_ref, keep_ref, send_ref):
    chip, core = spot[0], spot[1]
    depth = mine_ref.shape[0]
    x = jnp.concatenate([x_ref[chip ^ mask] for mask in masks], axis=0)
    low, high = x[:, :depth], x[:, depth:]
    here = jnp.full(low.shape, core, jnp.int32) == 0
    mine = jnp.where(here, low, high)
    beside = jnp.where(here, high, low)
    summed = jnp.dot(mine, mine_ref[...], preferred_element_type=jnp.float32) + jnp.dot(
        beside, beside_ref[...], preferred_element_type=jnp.float32
    )
    summed = summed.astype(jnp.bfloat16)
    half = summed.shape[0] // 2
    keep_ref[...] = summed[:half].reshape(keep_ref.shape)
    send_ref[...] = summed[half:].reshape(send_ref.shape)


def project(regrouped, mine, beside, spot, masks, part, parts):
    chips, rows, depth_pair = regrouped.shape
    depth, width = mine.shape
    columns = width // parts
    shape = jax.ShapeDtypeStruct((chips // 2, rows, columns), jnp.bfloat16)
    weight_spec = pl.BlockSpec((depth, columns), lambda i: (0, part))
    return pl.pallas_call(
        functools.partial(projection_kernel, masks),
        out_shape=[shape, shape],
        grid=(1,),
        in_specs=[
            SMEM,
            pl.BlockSpec((chips, rows, depth_pair), lambda i: (0, 0, 0)),
            weight_spec,
            weight_spec,
        ],
        out_specs=[pl.BlockSpec(shape.shape, lambda i: (0, 0, 0))] * 2,
        compiler_params=pltpu.CompilerParams(vmem_limit_bytes=16 << 20),
        cost_estimate=pl.CostEstimate(
            flops=270_000_000, bytes_accessed=1_800_000, transcendentals=0
        ),
        name=f"projection_{part}",
    )(spot, regrouped, mine, beside)


def dispatch_kernel(
    keep_a, got_a, keep_b, got_b, residual, gain, placing, hidden_ref, normed_ref, sent_ref
):
    rows = residual.shape[0]
    halves = []
    at = 0
    for keep, got in ((keep_a, got_a), (keep_b, got_b)):
        span = keep.shape[1]
        halves.append(
            residual[:, at : at + span].astype(jnp.float32)
            + (keep[...].astype(jnp.float32) + got[...].astype(jnp.float32))
        )
        at += span
    hidden = jnp.concatenate(halves, axis=1)
    hidden_ref[...] = hidden
    mean_square = jnp.mean(hidden * hidden, axis=1, keepdims=True)
    normed = (hidden * lax.rsqrt(mean_square + EPSILON) * gain[...]).astype(jnp.bfloat16)
    normed_ref[...] = normed
    blocks = at // BLOCK
    stacked = jnp.concatenate(
        [normed[:, i * BLOCK : (i + 1) * BLOCK] for i in range(blocks)], axis=0
    )
    step = 512
    for i in range(0, placing.shape[0], step):
        sent_ref[pl.ds(i, step), :] = jnp.dot(
            placing[pl.ds(i, step), :], stacked, preferred_element_type=jnp.float32
        ).astype(jnp.bfloat16)


def dispatch(keep_a, got_a, keep_b, got_b, residual, gain, placing):
    rows, width = residual.shape
    return pl.pallas_call(
        dispatch_kernel,
        out_shape=[
            jax.ShapeDtypeStruct((rows, width), jnp.float32),
            jax.ShapeDtypeStruct((rows, width), jnp.bfloat16),
            jax.ShapeDtypeStruct((placing.shape[0], BLOCK), jnp.bfloat16),
        ],
        in_specs=[VMEM] * 7,
        out_specs=[VMEM] * 3,
        compiler_params=pltpu.CompilerParams(vmem_limit_bytes=16 << 20),
        cost_estimate=pl.CostEstimate(
            flops=270_000_000, bytes_accessed=4_000_000, transcendentals=16
        ),
        name="dispatch",
    )(keep_a, got_a, keep_b, got_b, residual, gain, placing)


def turning(blocks, capacity, sources, back):
    lines = blocks * capacity * sources
    left = lax.broadcasted_iota(jnp.int32, (lines, lines), 0)
    right = lax.broadcasted_iota(jnp.int32, (lines, lines), 1)
    if back:
        left, right = right, left
    wanted = left % sources * (blocks * capacity) + left // sources
    return (wanted == right).astype(jnp.float32).astype(jnp.bfloat16)


def expert_kernel(
    arrived, gate_ref, up_ref, down_ref, out_ref, rows_in, rows_out, gate_sum, up_sum, hidden
):
    step = pl.program_id(0)
    groups, lines, _ = rows_in.shape
    blocks = pl.num_programs(0) // 2
    sources = arrived.shape[0] // groups
    each = lines // blocks
    capacity = each // sources

    @pl.when(step == 0)
    def _():
        turn = turning(blocks, capacity, sources, False)
        for g in range(groups):
            rows_in[g] = jnp.dot(
                turn,
                arrived[g * sources : (g + 1) * sources].reshape(lines, BLOCK),
                preferred_element_type=jnp.float32,
            ).astype(jnp.bfloat16)

    @pl.when(step < blocks)
    def _():
        at = pl.ds(pl.multiple_of(step * each, each), each)
        x = rows_in[:, at, :].reshape(groups * each, BLOCK)
        gate = jnp.dot(x, gate_ref[0], preferred_element_type=jnp.float32)
        up = jnp.dot(x, up_ref[0], preferred_element_type=jnp.float32)

        @pl.when(step == 0)
        def _():
            gate_sum[...] = gate
            up_sum[...] = up

        @pl.when(step > 0)
        def _():
            gate_sum[...] += gate
            up_sum[...] += up

    @pl.when(step == blocks - 1)
    def _():
        gate = gate_sum[...]
        hidden[...] = (gate / (1.0 + jnp.exp(-gate)) * up_sum[...]).astype(jnp.bfloat16)

    @pl.when(step >= blocks)
    def _():
        at = pl.ds(pl.multiple_of((step - blocks) * each, each), each)
        y = jnp.dot(hidden[...], down_ref[0], preferred_element_type=jnp.float32)
        rows_out[:, at, :] = y.astype(jnp.bfloat16).reshape(groups, each, BLOCK)

    @pl.when(step == 2 * blocks - 1)
    def _():
        turn = turning(blocks, capacity, sources, True)
        for g in range(groups):
            out_ref[g * sources : (g + 1) * sources] = (
                jnp.dot(turn, rows_out[g], preferred_element_type=jnp.float32)
                .astype(jnp.bfloat16)
                .reshape(sources, lines // sources, BLOCK)
            )


def run_expert(arrived, gate, up, down):
    experts, lines, _ = arrived.shape
    _, width, units = gate.shape
    blocks = width // BLOCK
    groups = 8
    capacity = lines // blocks
    token_rows = experts * capacity
    whole = pl.BlockSpec(arrived.shape, lambda i: (0, 0, 0))
    inward = pl.BlockSpec((1, BLOCK, units), lambda i: (0, jnp.minimum(i, blocks - 1), 0))
    turned = pltpu.VMEM((groups, experts // groups * lines, BLOCK), jnp.bfloat16)
    return pl.pallas_call(
        expert_kernel,
        out_shape=jax.ShapeDtypeStruct(arrived.shape, jnp.bfloat16),
        grid=(2 * blocks,),
        in_specs=[
            whole,
            inward,
            inward,
            pl.BlockSpec((1, units, BLOCK), lambda i: (0, 0, jnp.maximum(i - blocks, 0))),
        ],
        out_specs=whole,
        scratch_shapes=[
            turned,
            turned,
            pltpu.VMEM((token_rows, units), jnp.float32),
            pltpu.VMEM((token_rows, units), jnp.float32),
            pltpu.VMEM((token_rows, units), jnp.bfloat16),
        ],
        compiler_params=pltpu.CompilerParams(vmem_limit_bytes=40 << 20),
        cost_estimate=pl.CostEstimate(
            flops=5_900_000_000, bytes_accessed=23_000_000, transcendentals=200_000
        ),
        name="expert",
    )(arrived, gate, up, down)


def combine_kernel(mixing, returned, hidden, out_ref):
    rows = hidden.shape[0]
    mixed = jnp.dot(mixing[...], returned[...], preferred_element_type=jnp.float32)
    half = mixed.shape[0] // 2
    mixed = mixed[:half] + mixed[half:]
    for i in range(half // rows):
        lanes = slice(i * BLOCK, (i + 1) * BLOCK)
        out_ref[:, lanes] = (hidden[:, lanes] + mixed[i * rows : (i + 1) * rows]).astype(
            jnp.bfloat16
        )


def combine(mixing, returned, hidden):
    return pl.pallas_call(
        combine_kernel,
        out_shape=jax.ShapeDtypeStruct(hidden.shape, jnp.bfloat16),
        in_specs=[VMEM] * 3,
        out_specs=VMEM,
        compiler_params=pltpu.CompilerParams(vmem_limit_bytes=16 << 20),
        cost_estimate=pl.CostEstimate(
            flops=540_000_000, bytes_accessed=3_500_000, transcendentals=0
        ),
        name="combine",
    )(mixing, returned, hidden)


def route_gates(logits, routes):
    matches = routes[:, :, None] == jnp.arange(logits.shape[1], dtype=jnp.int32)[None, None, :]
    chosen = jnp.sum(jnp.where(matches, logits[:, None, :], 0.0), axis=-1)
    raised = jnp.exp(chosen)
    return raised / jnp.sum(raised, axis=1, keepdims=True)


def rank_of(flat_routes, experts):
    onehot = (flat_routes[:, None] == jnp.arange(experts, dtype=jnp.int32)[None, :]).astype(
        jnp.int32
    )
    earlier = jnp.cumsum(onehot, axis=0) - onehot
    return jnp.sum(earlier * onehot, axis=1)


def add(left, right):
    return (left.astype(jnp.float32) + right.astype(jnp.float32)).astype(jnp.bfloat16)


def scatter_sum(regrouped, mine, beside, spot, peers):
    jump = {"y": 1, "Y": 3, "z": 4, "Z": 12}

    def swap(array, way):
        return lax.ppermute(array, "dev", [(i, i ^ (2 * jump[way])) for i in range(peers)])

    orders = ("yYzZ", "YyzZ", "zZyY", "ZzyY")
    kept, got = [], []
    for part, order in enumerate(orders):
        masks = []
        for place in range(16):
            mask = 0
            for bit, way in enumerate(order):
                if place >> (3 - bit) & 1:
                    mask ^= jump[way]
            masks.append(mask)
        keep, send = project(regrouped, mine, beside, spot, tuple(masks), part, len(orders))
        kept.append(keep)
        got.append(swap(send, order[0]))
    for part, order in enumerate(orders):
        both = add(kept[part], got[part])
        half = both.shape[0] // 2
        kept[part], got[part] = both[:half], swap(both[half:], order[1])
    merged = []
    for pair in (0, 2):
        way, last = orders[pair][2:]
        both = jnp.concatenate(
            [add(kept[pair], got[pair]), add(kept[pair + 1], got[pair + 1])], axis=2
        )
        merged.append((both[:2], swap(both[2:], way), last))
    ends = []
    for keep, arrived, last in merged:
        both = add(keep, arrived)
        ends += [both[0], swap(both[1], last)]
    return ends


def shards(
    queries,
    new_keys,
    new_values,
    key_pages,
    value_pages,
    block_tables,
    context_lengths,
    out_weight,
    residual,
    norm_gain,
    router_weight,
    routes,
    expert_gate,
    expert_up,
    expert_down,
):
    rows, width = residual.shape
    peers = lax.axis_size("dev")
    chips = peers // 2
    place = lax.axis_index("dev")
    spot = jnp.stack([place // 2, place % 2])
    same_core = [[2 * chip + side for chip in range(chips)] for side in range(2)]
    experts = router_weight.shape[1]
    capacity = 2
    blocks = width // BLOCK
    lines = blocks * capacity

    weight_beside = lax.ppermute(out_weight, "dev", [(i, i ^ 1) for i in range(peers)])
    attended = attend(
        queries,
        new_keys,
        new_values,
        key_pages,
        value_pages,
        block_tables,
        context_lengths,
        chips,
    )
    regrouped = lax.all_to_all(
        attended, "dev", split_axis=0, concat_axis=0, axis_index_groups=same_core, tiled=True
    )
    ends = scatter_sum(regrouped, out_weight, weight_beside, spot, peers)

    rank = rank_of(routes.reshape(-1), experts).reshape(rows, -1)
    block_ids = jnp.arange(blocks, dtype=jnp.int32)
    target = (routes * lines + rank)[None] + (block_ids * capacity)[:, None, None]
    target = target.reshape(blocks * rows, -1)
    line = jnp.arange(experts * lines, dtype=jnp.int32)
    placed = line[:, None] == target[:, 0][None, :]
    for k in range(1, target.shape[1]):
        placed = placed | (line[:, None] == target[:, k][None, :])
    placing = placed.astype(jnp.bfloat16)

    hidden_state, normed, sent = dispatch(*ends, residual, norm_gain[None], placing)
    arrived = lax.all_to_all(
        sent.reshape(experts, lines, BLOCK),
        ("attn", "dev"),
        split_axis=0,
        concat_axis=0,
        tiled=True,
    )
    output_rows = run_expert(arrived, expert_gate, expert_up, expert_down)
    returned = lax.all_to_all(
        output_rows, ("attn", "dev"), split_axis=0, concat_axis=0, tiled=True
    ).reshape(experts * lines, BLOCK)

    logits = jnp.dot(normed, router_weight, preferred_element_type=jnp.float32)
    gate_values = route_gates(logits, routes)
    gate_of = jnp.tile(gate_values, (blocks, 1))
    mixing = jnp.zeros((blocks * rows, experts * lines), jnp.float32)
    for k in range(target.shape[1]):
        mixing = jnp.where(line[None, :] == target[:, k][:, None], gate_of[:, k][:, None], mixing)
    high = mixing.astype(jnp.bfloat16)
    low = (mixing - high.astype(jnp.float32)).astype(jnp.bfloat16)
    return combine(jnp.concatenate([high, low], axis=0), returned, hidden_state)


def solution(mesh):
    in_specs = (
        P(("attn", "dev"), None),
        P(("attn", "dev"), None),
        P(("attn", "dev"), None),
        P(("attn", "dev"), None, None),
        P(("attn", "dev"), None, None),
        P(("attn", "dev"), None),
        P(("attn", "dev")),
        P("dev", None),
        P(("attn", "dev"), None),
        P(),
        P(),
        P(("attn", "dev"), None),
        P(("attn", "dev"), None, None),
        P(("attn", "dev"), None, None),
        P(("attn", "dev"), None, None),
    )
    out_specs = P(("attn", "dev"), None)
    return jax.shard_map(shards, mesh=mesh, in_specs=in_specs, out_specs=out_specs, check_vma=False)
```

```python
import functools
import math

import jax
import jax.numpy as jnp
from jax import lax
from jax.experimental import pallas as pl
from jax.experimental.pallas import tpu as pltpu
from jax.sharding import PartitionSpec as P

HEADS = 64
KVH = 4
HD = 128
GROUP = HEADS // KVH
MAXCTX = 64
PAGE = 16
EPSILON = 1e-06
BLOCK = 512
ROWS = 32
TOGETHER = 4
CONTRACT_LAST = (((1,), (1,)), ((), ()))
VMEM = pl.BlockSpec(memory_space=pltpu.VMEM)
SMEM = pl.BlockSpec(memory_space=pltpu.SMEM)
HBM = pl.BlockSpec(memory_space=pltpu.HBM)


def attention_kernel(
    tables_far,
    lengths_far,
    q_far,
    own_key_far,
    own_value_far,
    keys_far,
    values_far,
    out_far,
    tables,
    lengths,
    q_near,
    own_key,
    own_value,
    keys,
    values,
    q_turned,
    out_turned,
    scores_held,
    own_held,
    weights_held,
    own_weights_held,
    out_near,
    sems,
    out_sems,
):
    rows = q_near.shape[0]
    pages = MAXCTX // PAGE
    tall, wide = TOGETHER * GROUP, TOGETHER * MAXCTX
    big = tall * KVH
    scale = 1.0 / math.sqrt(HD)
    inward = [
        pltpu.make_async_copy(far, near, sems.at[i])
        for i, (far, near) in enumerate(
            (
                (q_far, q_near),
                (own_key_far, own_key),
                (keys_far, keys),
                (values_far, values),
                (own_value_far, own_value),
                (tables_far, tables),
                (lengths_far, lengths),
            )
        )
    ]
    for copy in inward:
        copy.start()
    inward[0].wait()
    for head in range(HEADS):
        q_turned[head // GROUP, pl.ds(head % GROUP * rows, rows), :] = q_near[
            :, head * HD : (head + 1) * HD
        ].astype(jnp.float32)
    inward[1].wait()
    inward[2].wait()
    inward[5].wait()
    inward[6].wait()
    for first in range(0, rows, TOGETHER):
        page_ids = [tables[j, first + i] for i in range(TOGETHER) for j in range(pages)]
        for kv in range(KVH):
            lanes = slice(kv * HD, (kv + 1) * HD)
            q = jnp.concatenate(
                [
                    q_turned[kv, pl.ds(first + i, GROUP, stride=rows), :]
                    for i in range(TOGETHER)
                ],
                axis=0,
            ).astype(jnp.bfloat16)
            k = jnp.concatenate([keys[page, :, lanes] for page in page_ids], axis=0)
            at = pl.ds(first // TOGETHER * big + kv * tall, tall)
            scores_held[at, :] = (
                lax.dot_general(q, k, CONTRACT_LAST, preferred_element_type=jnp.float32) * scale
            )
            own_held[at, :] = (
                lax.dot_general(
                    q, own_key[:, lanes], CONTRACT_LAST, preferred_element_type=jnp.float32
                )
                * scale
            )
    row_request = lax.broadcasted_iota(jnp.int32, (big, wide), 0) // GROUP % TOGETHER
    place = lax.broadcasted_iota(jnp.int32, (big, wide), 1) - row_request * MAXCTX
    own_request = lax.broadcasted_iota(jnp.int32, (big, rows), 0) // GROUP % TOGETHER
    own_column = lax.broadcasted_iota(jnp.int32, (big, rows), 1)
    for first in range(0, rows, TOGETHER):
        at = pl.ds(first // TOGETHER * big, big)
        limit = jnp.zeros((big, wide), jnp.int32)
        for i in range(TOGETHER):
            limit = jnp.where(row_request == i, lengths[first + i], limit)
        scores = jnp.where((place >= 0) & (place < limit), scores_held[at, :], -jnp.inf)
        own_score = jnp.where(own_column == own_request + first, own_held[at, :], -jnp.inf)
        top = jnp.maximum(
            jnp.max(scores, axis=1, keepdims=True), jnp.max(own_score, axis=1, keepdims=True)
        )
        weights = jnp.exp(scores - top)
        own_weights = jnp.exp(own_score - top)
        share = 1.0 / (
            jnp.sum(weights, axis=1, keepdims=True) + jnp.sum(own_weights, axis=1, keepdims=True)
        )
        weights_held[at, :] = (weights * share).astype(jnp.bfloat16)
        own_weights_held[at, :] = (own_weights * share).astype(jnp.bfloat16)
    inward[3].wait()
    inward[4].wait()
    outward = []
    held = out_near.shape[2] // HD
    span = GROUP // held
    for kv in range(KVH):
        lanes = slice(kv * HD, (kv + 1) * HD)
        for first in range(0, rows, TOGETHER):
            page_ids = [tables[j, first + i] for i in range(TOGETHER) for j in range(pages)]
            at = pl.ds(first // TOGETHER * big + kv * tall, tall)
            v = jnp.concatenate([values[page, :, lanes] for page in page_ids], axis=0)
            blended = jnp.dot(
                weights_held[at, :], v, preferred_element_type=jnp.float32
            ) + jnp.dot(
                own_weights_held[at, :], own_value[:, lanes], preferred_element_type=jnp.float32
            )
            for i in range(TOGETHER):
                out_turned[kv, pl.ds(first + i, GROUP, stride=rows), :] = blended[
                    i * GROUP : (i + 1) * GROUP
                ]
        for head in range(kv * GROUP, (kv + 1) * GROUP):
            out_near[head // held, :, head % held * HD : (head % held + 1) * HD] = out_turned[
                kv, pl.ds(head % GROUP * rows, rows), :
            ].astype(jnp.bfloat16)
        part = pl.ds(kv * span, span)
        copy = pltpu.make_async_copy(out_near.at[part], out_far.at[part], out_sems.at[kv])
        copy.start()
        outward.append(copy)
    for copy in outward:
        copy.wait()


def attend(queries, new_keys, new_values, key_pool, value_pool, tables, lengths, chips):
    rows = queries.shape[0]
    total = HEADS * rows
    shape = (chips, rows, HEADS * HD // chips)
    wide = TOGETHER * MAXCTX
    bf16, f32 = jnp.bfloat16, jnp.float32
    return pl.pallas_call(
        attention_kernel,
        out_shape=pltpu.HBM(shape, bf16),
        in_specs=[HBM] * 7,
        out_specs=HBM,
        scratch_shapes=[
            pltpu.SMEM(tables.shape[::-1], jnp.int32),
            pltpu.SMEM(lengths.shape, jnp.int32),
            pltpu.VMEM(queries.shape, bf16),
            pltpu.VMEM(new_keys.shape, bf16),
            pltpu.VMEM(new_values.shape, bf16),
            pltpu.VMEM(key_pool.shape, bf16),
            pltpu.VMEM(value_pool.shape, bf16),
            pltpu.VMEM((KVH, GROUP * rows, HD), f32),
            pltpu.VMEM((KVH, GROUP * rows, HD), f32),
            pltpu.VMEM((total, wide), f32),
            pltpu.VMEM((total, rows), f32),
            pltpu.VMEM((total, wide), bf16),
            pltpu.VMEM((total, rows), bf16),
            pltpu.VMEM(shape, bf16),
            pltpu.SemaphoreType.DMA((7,)),
            pltpu.SemaphoreType.DMA((KVH,)),
        ],
        compiler_params=pltpu.CompilerParams(vmem_limit_bytes=12 << 20),
        cost_estimate=pl.CostEstimate(
            flops=600_000_000, bytes_accessed=5_000_000, transcendentals=300_000
        ),
        name="attention",
    )(
        *(
            pltpu.with_memory_space_constraint(array, pltpu.HBM)
            for array in (
                tables.T,
                lengths,
                queries,
                new_keys,
                new_values,
                key_pool,
                value_pool,
            )
        )
    )


def projection_kernel(orders, spot, x_ref, mine_far, beside_far, *refs):
    parts = len(orders)
    outs, weights, sems = refs[:parts], refs[parts], refs[parts + 1]
    chip, core = spot[0], spot[1]
    depth = mine_far.shape[0]
    _, rows, columns = outs[0].shape
    copies = []
    for i in range(parts):
        lanes = pl.ds(i * columns, columns)
        for j, (far, half) in enumerate(((mine_far, core), (beside_far, 1 - core))):
            at = pl.ds(pl.multiple_of(half * depth, depth), depth)
            copies.append(
                pltpu.make_async_copy(far.at[:, lanes], weights.at[i, at, :], sems.at[i, j])
            )
    ahead = 4
    for copy in copies[:ahead]:
        copy.start()
    for i, masks in enumerate(orders):
        x = jnp.concatenate([x_ref[chip ^ mask] for mask in masks], axis=0)
        copies[2 * i].wait()
        copies[2 * i + 1].wait()
        for copy in copies[2 * i + ahead : 2 * i + ahead + 2]:
            copy.start()
        outs[i][...] = (
            jnp.dot(x, weights[i], preferred_element_type=jnp.float32)
            .astype(jnp.bfloat16)
            .reshape(outs[i].shape)
        )


def project(regrouped, mine, beside, spot, orders, name):
    _, rows, depth = regrouped.shape
    parts = len(orders)
    columns = mine.shape[1] // parts
    return pl.pallas_call(
        functools.partial(projection_kernel, orders),
        out_shape=[
            jax.ShapeDtypeStruct((len(masks), rows, columns), jnp.bfloat16) for masks in orders
        ],
        in_specs=[SMEM, VMEM, HBM, HBM],
        out_specs=[VMEM] * parts,
        scratch_shapes=[
            pltpu.VMEM((parts, depth, columns), jnp.bfloat16),
            pltpu.SemaphoreType.DMA((parts, 2)),
        ],
        compiler_params=pltpu.CompilerParams(vmem_limit_bytes=12 << 20),
        cost_estimate=pl.CostEstimate(
            flops=540_000_000, bytes_accessed=5_500_000, transcendentals=0
        ),
        name=name,
    )(
        spot,
        regrouped,
        pltpu.with_memory_space_constraint(mine, pltpu.HBM),
        pltpu.with_memory_space_constraint(beside, pltpu.HBM),
    )


def dispatch_kernel(
    keep_a,
    got_a,
    keep_b,
    got_b,
    residual,
    gain,
    placing,
    hidden_far,
    normed_far,
    sent_ref,
    hidden_ref,
    normed_ref,
    sems,
):
    rows = residual.shape[0]
    halves = []
    at = 0
    for keep, got in ((keep_a, got_a), (keep_b, got_b)):
        span = keep.shape[1]
        halves.append(
            residual[:, at : at + span].astype(jnp.float32)
            + (keep[...].astype(jnp.float32) + got[...].astype(jnp.float32))
        )
        at += span
    hidden = jnp.concatenate(halves, axis=1)
    hidden_ref[...] = hidden
    mean_square = jnp.mean(hidden * hidden, axis=1, keepdims=True)
    normed = (hidden * lax.rsqrt(mean_square + EPSILON) * gain[...]).astype(jnp.bfloat16)
    normed_ref[...] = normed
    copies = [
        pltpu.make_async_copy(hidden_ref, hidden_far, sems.at[0]),
        pltpu.make_async_copy(normed_ref, normed_far, sems.at[1]),
    ]
    for copy in copies:
        copy.start()
    blocks = at // BLOCK
    stacked = jnp.concatenate(
        [normed[:, i * BLOCK : (i + 1) * BLOCK] for i in range(blocks)], axis=0
    )
    step = 512
    for i in range(0, placing.shape[0], step):
        part = pl.ds(i, step)
        sent_ref[part, :] = jnp.dot(
            placing[part, :], stacked, preferred_element_type=jnp.float32
        ).astype(jnp.bfloat16)
    for copy in copies:
        copy.wait()


def dispatch(keep_a, got_a, keep_b, got_b, residual, gain, placing):
    rows, width = residual.shape
    return pl.pallas_call(
        dispatch_kernel,
        out_shape=[
            pltpu.HBM((rows, width), jnp.float32),
            pltpu.HBM((rows, width), jnp.bfloat16),
            jax.ShapeDtypeStruct((placing.shape[0], BLOCK), jnp.bfloat16),
        ],
        in_specs=[VMEM] * 7,
        out_specs=[HBM, HBM, VMEM],
        scratch_shapes=[
            pltpu.VMEM((rows, width), jnp.float32),
            pltpu.VMEM((rows, width), jnp.bfloat16),
            pltpu.SemaphoreType.DMA((2,)),
        ],
        compiler_params=pltpu.CompilerParams(vmem_limit_bytes=8 << 20),
        cost_estimate=pl.CostEstimate(
            flops=270_000_000, bytes_accessed=4_000_000, transcendentals=16
        ),
        name="dispatch",
    )(keep_a, got_a, keep_b, got_b, residual, gain, placing)


def turning(blocks, capacity, sources, back):
    lines = blocks * capacity * sources
    left = lax.broadcasted_iota(jnp.int32, (lines, lines), 0)
    right = lax.broadcasted_iota(jnp.int32, (lines, lines), 1)
    if back:
        left, right = right, left
    wanted = left % sources * (blocks * capacity) + left // sources
    return (wanted == right).astype(jnp.float32).astype(jnp.bfloat16)


def rows_kernel(arrived, out_ref):
    groups = out_ref.shape[0] // ROWS
    sources = arrived.shape[0] // groups
    blocks = out_ref.shape[1] // BLOCK
    lines = arrived.shape[1] * sources
    turn = turning(blocks, arrived.shape[1] // blocks, sources, False)
    for g in range(groups):
        turned = jnp.dot(
            turn,
            arrived[g * sources : (g + 1) * sources].reshape(lines, BLOCK),
            preferred_element_type=jnp.float32,
        ).astype(jnp.bfloat16)
        for i in range(blocks):
            out_ref[g * ROWS : (g + 1) * ROWS, i * BLOCK : (i + 1) * BLOCK] = turned[
                i * ROWS : (i + 1) * ROWS
            ]


def lines_kernel(rows_ref, out_far, out_near, sems):
    groups = rows_ref.shape[0] // ROWS
    blocks = rows_ref.shape[1] // BLOCK
    sources = out_near.shape[0] // groups
    turn = turning(blocks, out_near.shape[1] // blocks, sources, True)
    outward = []
    for g in range(groups):
        part = pl.ds(g * sources, sources)
        stacked = jnp.concatenate(
            [
                rows_ref[g * ROWS : (g + 1) * ROWS, i * BLOCK : (i + 1) * BLOCK]
                for i in range(blocks)
            ],
            axis=0,
        )
        out_near[part] = (
            jnp.dot(turn, stacked, preferred_element_type=jnp.float32)
            .astype(jnp.bfloat16)
            .reshape(sources, out_near.shape[1], BLOCK)
        )
        copy = pltpu.make_async_copy(out_near.at[part], out_far.at[part], sems.at[g])
        copy.start()
        outward.append(copy)
    for copy in outward:
        copy.wait()


def run_expert(arrived, gate, up, down):
    experts, lines, _ = arrived.shape
    width = gate.shape[0]
    token_rows = experts * lines // (width // BLOCK)
    groups = token_rows // ROWS
    params = pltpu.CompilerParams(vmem_limit_bytes=12 << 20)
    cost = pl.CostEstimate(flops=540_000_000, bytes_accessed=4_200_000, transcendentals=0)
    rows = pl.pallas_call(
        rows_kernel,
        out_shape=jax.ShapeDtypeStruct((token_rows, width), jnp.bfloat16),
        in_specs=[VMEM],
        out_specs=VMEM,
        compiler_params=params,
        cost_estimate=cost,
        name="slots_to_rows",
    )(arrived)
    gate_part = jnp.dot(rows, gate, preferred_element_type=jnp.float32)
    gate_part, up = lax.optimization_barrier((gate_part, up))
    up_part = jnp.dot(rows, up, preferred_element_type=jnp.float32)
    expert_hidden, down = lax.optimization_barrier(
        ((jax.nn.silu(gate_part) * up_part).astype(jnp.bfloat16), down)
    )
    output = jnp.dot(expert_hidden, down, preferred_element_type=jnp.float32).astype(jnp.bfloat16)
    return pl.pallas_call(
        lines_kernel,
        out_shape=pltpu.HBM(arrived.shape, jnp.bfloat16),
        in_specs=[VMEM],
        out_specs=HBM,
        scratch_shapes=[
            pltpu.VMEM(arrived.shape, jnp.bfloat16),
            pltpu.SemaphoreType.DMA((groups,)),
        ],
        compiler_params=params,
        cost_estimate=cost,
        name="rows_to_slots",
    )(output)


def mixing_kernel(target, gate_of, high_far, low_far, high_ref, low_ref, sems):
    tall, wide = high_ref.shape
    step = 256
    for at in range(0, wide, step):
        line = lax.broadcasted_iota(jnp.int32, (tall, step), 1) + at
        mixing = jnp.zeros((tall, step), jnp.float32)
        for k in range(target.shape[1]):
            mixing = jnp.where(line == target[:, k : k + 1], gate_of[:, k : k + 1], mixing)
        high = mixing.astype(jnp.bfloat16)
        high_ref[:, at : at + step] = high
        low_ref[:, at : at + step] = (mixing - high.astype(jnp.float32)).astype(jnp.bfloat16)
    copies = [
        pltpu.make_async_copy(high_ref, high_far, sems.at[0]),
        pltpu.make_async_copy(low_ref, low_far, sems.at[1]),
    ]
    for copy in copies:
        copy.start()
    for copy in copies:
        copy.wait()


def mix(target, gate_of, lines):
    shape = (target.shape[0], lines)
    return pl.pallas_call(
        mixing_kernel,
        out_shape=[pltpu.HBM(shape, jnp.bfloat16)] * 2,
        in_specs=[VMEM, VMEM],
        out_specs=[HBM, HBM],
        scratch_shapes=[
            pltpu.VMEM(shape, jnp.bfloat16),
            pltpu.VMEM(shape, jnp.bfloat16),
            pltpu.SemaphoreType.DMA((2,)),
        ],
        compiler_params=pltpu.CompilerParams(vmem_limit_bytes=8 << 20),
        cost_estimate=pl.CostEstimate(flops=6_000_000, bytes_accessed=1_200_000, transcendentals=0),
        name="mixing",
    )(target, gate_of)


def combine_kernel(high_far, low_far, returned, hidden_far, out_ref, mixing, hidden, sems):
    rows = hidden.shape[0]
    half = high_far.shape[0]
    copies = [
        pltpu.make_async_copy(high_far, mixing.at[pl.ds(0, half)], sems.at[0]),
        pltpu.make_async_copy(low_far, mixing.at[pl.ds(half, half)], sems.at[1]),
        pltpu.make_async_copy(hidden_far, hidden, sems.at[2]),
    ]
    for copy in copies:
        copy.start()
    for copy in copies:
        copy.wait()
    mixed = jnp.dot(mixing[...], returned[...], preferred_element_type=jnp.float32)
    mixed = mixed[:half] + mixed[half:]
    for i in range(half // rows):
        lanes = slice(i * BLOCK, (i + 1) * BLOCK)
        out_ref[:, lanes] = (hidden[:, lanes] + mixed[i * rows : (i + 1) * rows]).astype(
            jnp.bfloat16
        )


def combine(high, low, returned, hidden):
    far = [pltpu.with_memory_space_constraint(array, pltpu.HBM) for array in (high, low, hidden)]
    return pl.pallas_call(
        combine_kernel,
        out_shape=jax.ShapeDtypeStruct(hidden.shape, jnp.bfloat16),
        in_specs=[HBM, HBM, VMEM, HBM],
        out_specs=VMEM,
        scratch_shapes=[
            pltpu.VMEM((2 * high.shape[0], high.shape[1]), jnp.bfloat16),
            pltpu.VMEM(hidden.shape, jnp.float32),
            pltpu.SemaphoreType.DMA((3,)),
        ],
        compiler_params=pltpu.CompilerParams(vmem_limit_bytes=8 << 20),
        cost_estimate=pl.CostEstimate(
            flops=540_000_000, bytes_accessed=3_500_000, transcendentals=0
        ),
        name="combine",
    )(far[0], far[1], returned, far[2])


def route_gates(logits, routes):
    matches = routes[:, :, None] == jnp.arange(logits.shape[1], dtype=jnp.int32)[None, None, :]
    chosen = jnp.sum(jnp.where(matches, logits[:, None, :], 0.0), axis=-1)
    raised = jnp.exp(chosen)
    return raised / jnp.sum(raised, axis=1, keepdims=True)


def rank_of(flat_routes, experts):
    onehot = (flat_routes[:, None] == jnp.arange(experts, dtype=jnp.int32)[None, :]).astype(
        jnp.int32
    )
    earlier = jnp.cumsum(onehot, axis=0) - onehot
    return jnp.sum(earlier * onehot, axis=1)


def add(left, right):
    return (left.astype(jnp.float32) + right.astype(jnp.float32)).astype(jnp.bfloat16)


def scatter_sum(regrouped, mine, beside, spot, peers):
    jump = {"y": 1, "Y": 3, "z": 4, "Z": 12}

    def swap(array, way):
        return lax.ppermute(array, "dev", [(i, i ^ (2 * jump[way])) for i in range(peers)])

    orders = ("yYzZ", "YyzZ", "zZyY", "ZzyY")
    masks = []
    for order in orders:
        places = []
        for place in range(16):
            mask = 0
            for bit, way in enumerate(order):
                if place >> (3 - bit) & 1:
                    mask ^= jump[way]
            places.append(mask)
        masks.append(tuple(places))
    sent = project(regrouped, mine, beside, spot, [places[8:] for places in masks], "project_sent")
    got = [swap(array, order[0]) for array, order in zip(sent, orders)]
    regrouped, _ = lax.optimization_barrier((regrouped, sent[0]))
    kept = list(
        project(regrouped, mine, beside, spot, [places[:8] for places in masks], "project_kept")
    )
    for part, order in enumerate(orders):
        both = add(kept[part], got[part])
        half = both.shape[0] // 2
        kept[part], got[part] = both[:half], swap(both[half:], order[1])
    merged = []
    for pair in (0, 2):
        way, last = orders[pair][2:]
        both = jnp.concatenate(
            [add(kept[pair], got[pair]), add(kept[pair + 1], got[pair + 1])], axis=2
        )
        merged.append((both[:2], swap(both[2:], way), last))
    ends = []
    for keep, arrived, last in merged:
        both = add(keep, arrived)
        ends += [both[0], swap(both[1], last)]
    return ends


def shards(
    queries,
    new_keys,
    new_values,
    key_pages,
    value_pages,
    block_tables,
    context_lengths,
    out_weight,
    residual,
    norm_gain,
    router_weight,
    routes,
    expert_gate,
    expert_up,
    expert_down,
):
    rows, width = residual.shape
    peers = lax.axis_size("dev")
    chips = peers // 2
    place = lax.axis_index("dev")
    same_core = [[2 * chip + side for chip in range(chips)] for side in range(2)]
    experts = router_weight.shape[1]
    capacity = 2
    blocks = width // BLOCK
    lines = blocks * capacity

    weight_beside = lax.ppermute(out_weight, "dev", [(i, i ^ 1) for i in range(peers)])
    attended = attend(
        queries,
        new_keys,
        new_values,
        key_pages,
        value_pages,
        block_tables,
        context_lengths,
        chips,
    )
    regrouped = lax.all_to_all(
        attended, "dev", split_axis=0, concat_axis=0, axis_index_groups=same_core, tiled=True
    )
    spot = jnp.stack([place // 2, place % 2])
    ends = scatter_sum(regrouped, out_weight, weight_beside, spot, peers)

    rank = rank_of(routes.reshape(-1), experts).reshape(rows, -1)
    block_ids = jnp.arange(blocks, dtype=jnp.int32)
    target = (routes * lines + rank)[None] + (block_ids * capacity)[:, None, None]
    target = target.reshape(blocks * rows, -1)
    line = jnp.arange(experts * lines, dtype=jnp.int32)
    placed = line[:, None] == target[:, 0][None, :]
    for k in range(1, target.shape[1]):
        placed = placed | (line[:, None] == target[:, k][None, :])
    placing = placed.astype(jnp.bfloat16)

    hidden_state, normed, sent = dispatch(*ends, residual, norm_gain[None], placing)
    arrived = lax.all_to_all(
        sent.reshape(experts, lines, BLOCK),
        ("attn", "dev"),
        split_axis=0,
        concat_axis=0,
        tiled=True,
    )
    output_rows = run_expert(arrived, expert_gate[0], expert_up[0], expert_down[0])
    returned = lax.all_to_all(
        output_rows, ("attn", "dev"), split_axis=0, concat_axis=0, tiled=True
    ).reshape(experts * lines, BLOCK)

    logits = jnp.dot(normed, router_weight, preferred_element_type=jnp.float32)
    gate_values = route_gates(logits, routes)
    gate_of = jnp.tile(gate_values, (blocks, 1))
    high, low = mix(target, gate_of, experts * lines)
    return combine(high, low, returned, hidden_state)


def solution(mesh):
    in_specs = (
        P(("attn", "dev"), None),
        P(("attn", "dev"), None),
        P(("attn", "dev"), None),
        P(("attn", "dev"), None, None),
        P(("attn", "dev"), None, None),
        P(("attn", "dev"), None),
        P(("attn", "dev")),
        P("dev", None),
        P(("attn", "dev"), None),
        P(),
        P(),
        P(("attn", "dev"), None),
        P(("attn", "dev"), None, None),
        P(("attn", "dev"), None, None),
        P(("attn", "dev"), None, None),
    )
    out_specs = P(("attn", "dev"), None)
    return jax.shard_map(shards, mesh=mesh, in_specs=in_specs, out_specs=out_specs, check_vma=False)
```

```python
import functools
import math

import jax
import jax.numpy as jnp
from jax import lax
from jax.experimental import pallas as pl
from jax.experimental.pallas import tpu as pltpu
from jax.sharding import PartitionSpec as P

HEADS = 64
KVH = 4
HD = 128
GROUP = HEADS // KVH
MAXCTX = 64
PAGE = 16
EPSILON = 1e-06
BLOCK = 512
ROWS = 32
TOGETHER = 4
CONTRACT_LAST = (((1,), (1,)), ((), ()))
VMEM = pl.BlockSpec(memory_space=pltpu.VMEM)
SMEM = pl.BlockSpec(memory_space=pltpu.SMEM)
HBM = pl.BlockSpec(memory_space=pltpu.HBM)


def attention_kernel(
    tables_far,
    lengths_far,
    q_far,
    own_key_far,
    own_value_far,
    keys_far,
    values_far,
    out_far,
    tables,
    lengths,
    q_near,
    own_key,
    own_value,
    keys,
    values,
    q_turned,
    out_turned,
    scores_held,
    own_held,
    weights_held,
    own_weights_held,
    out_near,
    sems,
    out_sems,
):
    rows = q_near.shape[0]
    pages = MAXCTX // PAGE
    tall, wide = TOGETHER * GROUP, TOGETHER * MAXCTX
    big = tall * KVH
    scale = 1.0 / math.sqrt(HD)
    inward = [
        pltpu.make_async_copy(far, near, sems.at[i])
        for i, (far, near) in enumerate(
            (
                (q_far, q_near),
                (own_key_far, own_key),
                (keys_far, keys),
                (values_far, values),
                (own_value_far, own_value),
                (tables_far, tables),
                (lengths_far, lengths),
            )
        )
    ]
    for copy in inward:
        copy.start()
    inward[0].wait()
    for head in range(HEADS):
        q_turned[head // GROUP, pl.ds(head % GROUP * rows, rows), :] = q_near[
            :, head * HD : (head + 1) * HD
        ].astype(jnp.float32)
    inward[1].wait()
    inward[2].wait()
    inward[5].wait()
    inward[6].wait()
    for first in range(0, rows, TOGETHER):
        page_ids = [tables[j, first + i] for i in range(TOGETHER) for j in range(pages)]
        for kv in range(KVH):
            lanes = slice(kv * HD, (kv + 1) * HD)
            q = jnp.concatenate(
                [
                    q_turned[kv, pl.ds(first + i, GROUP, stride=rows), :]
                    for i in range(TOGETHER)
                ],
                axis=0,
            ).astype(jnp.bfloat16)
            k = jnp.concatenate([keys[page, :, lanes] for page in page_ids], axis=0)
            at = pl.ds(first // TOGETHER * big + kv * tall, tall)
            scores_held[at, :] = (
                lax.dot_general(q, k, CONTRACT_LAST, preferred_element_type=jnp.float32) * scale
            )
            own_held[at, :] = (
                lax.dot_general(
                    q, own_key[:, lanes], CONTRACT_LAST, preferred_element_type=jnp.float32
                )
                * scale
            )
    row_request = lax.broadcasted_iota(jnp.int32, (big, wide), 0) // GROUP % TOGETHER
    place = lax.broadcasted_iota(jnp.int32, (big, wide), 1) - row_request * MAXCTX
    own_request = lax.broadcasted_iota(jnp.int32, (big, rows), 0) // GROUP % TOGETHER
    own_column = lax.broadcasted_iota(jnp.int32, (big, rows), 1)
    for first in range(0, rows, TOGETHER):
        at = pl.ds(first // TOGETHER * big, big)
        limit = jnp.zeros((big, wide), jnp.int32)
        for i in range(TOGETHER):
            limit = jnp.where(row_request == i, lengths[first + i], limit)
        scores = jnp.where((place >= 0) & (place < limit), scores_held[at, :], -jnp.inf)
        own_score = jnp.where(own_column == own_request + first, own_held[at, :], -jnp.inf)
        top = jnp.maximum(
            jnp.max(scores, axis=1, keepdims=True), jnp.max(own_score, axis=1, keepdims=True)
        )
        weights = jnp.exp(scores - top)
        own_weights = jnp.exp(own_score - top)
        share = 1.0 / (
            jnp.sum(weights, axis=1, keepdims=True) + jnp.sum(own_weights, axis=1, keepdims=True)
        )
        weights_held[at, :] = (weights * share).astype(jnp.bfloat16)
        own_weights_held[at, :] = (own_weights * share).astype(jnp.bfloat16)
    inward[3].wait()
    inward[4].wait()
    outward = []
    held = out_near.shape[2] // HD
    span = GROUP // held
    for kv in range(KVH):
        lanes = slice(kv * HD, (kv + 1) * HD)
        for first in range(0, rows, TOGETHER):
            page_ids = [tables[j, first + i] for i in range(TOGETHER) for j in range(pages)]
            at = pl.ds(first // TOGETHER * big + kv * tall, tall)
            v = jnp.concatenate([values[page, :, lanes] for page in page_ids], axis=0)
            blended = jnp.dot(
                weights_held[at, :], v, preferred_element_type=jnp.float32
            ) + jnp.dot(
                own_weights_held[at, :], own_value[:, lanes], preferred_element_type=jnp.float32
            )
            for i in range(TOGETHER):
                out_turned[kv, pl.ds(first + i, GROUP, stride=rows), :] = blended[
                    i * GROUP : (i + 1) * GROUP
                ]
        for head in range(kv * GROUP, (kv + 1) * GROUP):
            out_near[head // held, :, head % held * HD : (head % held + 1) * HD] = out_turned[
                kv, pl.ds(head % GROUP * rows, rows), :
            ].astype(jnp.bfloat16)
        part = pl.ds(kv * span, span)
        copy = pltpu.make_async_copy(out_near.at[part], out_far.at[part], out_sems.at[kv])
        copy.start()
        outward.append(copy)
    for copy in outward:
        copy.wait()


def attend(queries, new_keys, new_values, key_pool, value_pool, tables, lengths, chips):
    rows = queries.shape[0]
    total = HEADS * rows
    shape = (chips, rows, HEADS * HD // chips)
    wide = TOGETHER * MAXCTX
    bf16, f32 = jnp.bfloat16, jnp.float32
    return pl.pallas_call(
        attention_kernel,
        out_shape=pltpu.HBM(shape, bf16),
        in_specs=[HBM] * 7,
        out_specs=HBM,
        scratch_shapes=[
            pltpu.SMEM(tables.shape[::-1], jnp.int32),
            pltpu.SMEM(lengths.shape, jnp.int32),
            pltpu.VMEM(queries.shape, bf16),
            pltpu.VMEM(new_keys.shape, bf16),
            pltpu.VMEM(new_values.shape, bf16),
            pltpu.VMEM(key_pool.shape, bf16),
            pltpu.VMEM(value_pool.shape, bf16),
            pltpu.VMEM((KVH, GROUP * rows, HD), f32),
            pltpu.VMEM((KVH, GROUP * rows, HD), f32),
            pltpu.VMEM((total, wide), f32),
            pltpu.VMEM((total, rows), f32),
            pltpu.VMEM((total, wide), bf16),
            pltpu.VMEM((total, rows), bf16),
            pltpu.VMEM(shape, bf16),
            pltpu.SemaphoreType.DMA((7,)),
            pltpu.SemaphoreType.DMA((KVH,)),
        ],
        compiler_params=pltpu.CompilerParams(vmem_limit_bytes=12 << 20),
        cost_estimate=pl.CostEstimate(
            flops=600_000_000, bytes_accessed=5_000_000, transcendentals=300_000
        ),
        name="attention",
    )(
        *(
            pltpu.with_memory_space_constraint(array, pltpu.HBM)
            for array in (
                tables.T,
                lengths,
                queries,
                new_keys,
                new_values,
                key_pool,
                value_pool,
            )
        )
    )


def projection_kernel(orders, spot, x_ref, mine, beside, *outs):
    chip, core = spot[0], spot[1]
    depth = mine.shape[0]
    columns = outs[0].shape[2]
    for i, (masks, out) in enumerate(zip(orders, outs)):
        lanes = slice(i * columns, (i + 1) * columns)
        x = jnp.concatenate([x_ref[chip ^ mask] for mask in masks], axis=0)
        low, high = x[:, :depth], x[:, depth:]
        here = jnp.full(low.shape, core, jnp.int32) == 0
        out[...] = (
            (
                jnp.dot(
                    jnp.where(here, low, high),
                    mine[:, lanes],
                    preferred_element_type=jnp.float32,
                )
                + jnp.dot(
                    jnp.where(here, high, low),
                    beside[:, lanes],
                    preferred_element_type=jnp.float32,
                )
            )
            .astype(jnp.bfloat16)
            .reshape(out.shape)
        )


def project(regrouped, mine, beside, spot, orders, name):
    _, rows, _ = regrouped.shape
    columns = mine.shape[1] // len(orders)
    return pl.pallas_call(
        functools.partial(projection_kernel, orders),
        out_shape=[
            jax.ShapeDtypeStruct((len(masks), rows, columns), jnp.bfloat16) for masks in orders
        ],
        in_specs=[SMEM, VMEM, VMEM, VMEM],
        out_specs=[VMEM] * len(orders),
        compiler_params=pltpu.CompilerParams(vmem_limit_bytes=8 << 20),
        cost_estimate=pl.CostEstimate(
            flops=540_000_000, bytes_accessed=5_500_000, transcendentals=0
        ),
        name=name,
    )(
        spot,
        regrouped,
        pltpu.with_memory_space_constraint(mine, pltpu.VMEM),
        pltpu.with_memory_space_constraint(beside, pltpu.VMEM),
    )


def dispatch_kernel(
    keep_a,
    got_a,
    keep_b,
    got_b,
    residual,
    gain,
    placing,
    hidden_far,
    normed_far,
    sent_ref,
    hidden_ref,
    normed_ref,
    sems,
):
    rows = residual.shape[0]
    halves = []
    at = 0
    for keep, got in ((keep_a, got_a), (keep_b, got_b)):
        span = keep.shape[1]
        halves.append(
            residual[:, at : at + span].astype(jnp.float32)
            + (keep[...].astype(jnp.float32) + got[...].astype(jnp.float32))
        )
        at += span
    hidden = jnp.concatenate(halves, axis=1)
    hidden_ref[...] = hidden
    mean_square = jnp.mean(hidden * hidden, axis=1, keepdims=True)
    normed = (hidden * lax.rsqrt(mean_square + EPSILON) * gain[...]).astype(jnp.bfloat16)
    normed_ref[...] = normed
    copies = [
        pltpu.make_async_copy(hidden_ref, hidden_far, sems.at[0]),
        pltpu.make_async_copy(normed_ref, normed_far, sems.at[1]),
    ]
    for copy in copies:
        copy.start()
    blocks = at // BLOCK
    stacked = jnp.concatenate(
        [normed[:, i * BLOCK : (i + 1) * BLOCK] for i in range(blocks)], axis=0
    )
    step = 512
    for i in range(0, placing.shape[0], step):
        part = pl.ds(i, step)
        sent_ref[part, :] = jnp.dot(
            placing[part, :], stacked, preferred_element_type=jnp.float32
        ).astype(jnp.bfloat16)
    for copy in copies:
        copy.wait()


def dispatch(keep_a, got_a, keep_b, got_b, residual, gain, placing):
    rows, width = residual.shape
    return pl.pallas_call(
        dispatch_kernel,
        out_shape=[
            pltpu.HBM((rows, width), jnp.float32),
            pltpu.HBM((rows, width), jnp.bfloat16),
            jax.ShapeDtypeStruct((placing.shape[0], BLOCK), jnp.bfloat16),
        ],
        in_specs=[VMEM] * 7,
        out_specs=[HBM, HBM, VMEM],
        scratch_shapes=[
            pltpu.VMEM((rows, width), jnp.float32),
            pltpu.VMEM((rows, width), jnp.bfloat16),
            pltpu.SemaphoreType.DMA((2,)),
        ],
        compiler_params=pltpu.CompilerParams(vmem_limit_bytes=8 << 20),
        cost_estimate=pl.CostEstimate(
            flops=270_000_000, bytes_accessed=4_000_000, transcendentals=16
        ),
        name="dispatch",
    )(keep_a, got_a, keep_b, got_b, residual, gain, placing)


def turning(blocks, capacity, sources, back):
    lines = blocks * capacity * sources
    left = lax.broadcasted_iota(jnp.int32, (lines, lines), 0)
    right = lax.broadcasted_iota(jnp.int32, (lines, lines), 1)
    if back:
        left, right = right, left
    wanted = left % sources * (blocks * capacity) + left // sources
    return (wanted == right).astype(jnp.float32).astype(jnp.bfloat16)


def expert_kernel(
    arrived, gate, up, down, out_far, rows_in, hidden, rows_out, out_near, sems
):
    groups = rows_out.shape[0]
    width = rows_in.shape[1]
    sources = arrived.shape[0] // groups
    blocks = width // BLOCK
    lines = arrived.shape[1] * sources
    each = lines // blocks
    capacity = arrived.shape[1] // blocks
    turn = turning(blocks, capacity, sources, False)
    for g in range(groups):
        turned = jnp.dot(
            turn,
            arrived[g * sources : (g + 1) * sources].reshape(lines, BLOCK),
            preferred_element_type=jnp.float32,
        ).astype(jnp.bfloat16)
        for i in range(blocks):
            rows_in[g * each : (g + 1) * each, i * BLOCK : (i + 1) * BLOCK] = turned[
                i * each : (i + 1) * each
            ]
    units = hidden.shape[1]
    step = 256
    for at in range(0, units, step):
        lanes = slice(at, at + step)
        gated = jnp.dot(rows_in[...], gate[0, :, lanes], preferred_element_type=jnp.float32)
        raised = jnp.dot(rows_in[...], up[0, :, lanes], preferred_element_type=jnp.float32)
        hidden[:, lanes] = (gated / (1.0 + jnp.exp(-gated)) * raised).astype(jnp.bfloat16)
    for i in range(blocks):
        lanes = slice(i * BLOCK, (i + 1) * BLOCK)
        output = jnp.dot(hidden[...], down[0, :, lanes], preferred_element_type=jnp.float32)
        rows_out[:, i * each : (i + 1) * each, :] = output.astype(jnp.bfloat16).reshape(
            groups, each, BLOCK
        )
    turn = turning(blocks, capacity, sources, True)
    outward = []
    for g in range(groups):
        part = pl.ds(g * sources, sources)
        out_near[part] = (
            jnp.dot(turn, rows_out[g], preferred_element_type=jnp.float32)
            .astype(jnp.bfloat16)
            .reshape(sources, arrived.shape[1], BLOCK)
        )
        copy = pltpu.make_async_copy(out_near.at[part], out_far.at[part], sems.at[g])
        copy.start()
        outward.append(copy)
    for copy in outward:
        copy.wait()


def run_expert(arrived, gate, up, down):
    experts, lines, _ = arrived.shape
    _, width, units = gate.shape
    token_rows = experts * lines // (width // BLOCK)
    groups = token_rows // ROWS
    return pl.pallas_call(
        expert_kernel,
        out_shape=pltpu.HBM(arrived.shape, jnp.bfloat16),
        in_specs=[VMEM] * 4,
        out_specs=HBM,
        scratch_shapes=[
            pltpu.VMEM((token_rows, width), jnp.bfloat16),
            pltpu.VMEM((token_rows, units), jnp.bfloat16),
            pltpu.VMEM((groups, token_rows, BLOCK), jnp.bfloat16),
            pltpu.VMEM(arrived.shape, jnp.bfloat16),
            pltpu.SemaphoreType.DMA((groups,)),
        ],
        compiler_params=pltpu.CompilerParams(vmem_limit_bytes=12 << 20),
        cost_estimate=pl.CostEstimate(
            flops=5_900_000_000, bytes_accessed=23_000_000, transcendentals=200_000
        ),
        name="expert",
    )(
        arrived,
        *(pltpu.with_memory_space_constraint(array, pltpu.VMEM) for array in (gate, up, down)),
    )


def mixing_kernel(target, gate_of, high_far, low_far, high_ref, low_ref, sems):
    tall, wide = high_ref.shape
    step = 256
    for at in range(0, wide, step):
        line = lax.broadcasted_iota(jnp.int32, (tall, step), 1) + at
        mixing = jnp.zeros((tall, step), jnp.float32)
        for k in range(target.shape[1]):
            mixing = jnp.where(line == target[:, k : k + 1], gate_of[:, k : k + 1], mixing)
        high = mixing.astype(jnp.bfloat16)
        high_ref[:, at : at + step] = high
        low_ref[:, at : at + step] = (mixing - high.astype(jnp.float32)).astype(jnp.bfloat16)
    copies = [
        pltpu.make_async_copy(high_ref, high_far, sems.at[0]),
        pltpu.make_async_copy(low_ref, low_far, sems.at[1]),
    ]
    for copy in copies:
        copy.start()
    for copy in copies:
        copy.wait()


def mix(target, gate_of, lines):
    shape = (target.shape[0], lines)
    return pl.pallas_call(
        mixing_kernel,
        out_shape=[pltpu.HBM(shape, jnp.bfloat16)] * 2,
        in_specs=[VMEM, VMEM],
        out_specs=[HBM, HBM],
        scratch_shapes=[
            pltpu.VMEM(shape, jnp.bfloat16),
            pltpu.VMEM(shape, jnp.bfloat16),
            pltpu.SemaphoreType.DMA((2,)),
        ],
        compiler_params=pltpu.CompilerParams(vmem_limit_bytes=8 << 20),
        cost_estimate=pl.CostEstimate(flops=6_000_000, bytes_accessed=1_200_000, transcendentals=0),
        name="mixing",
    )(target, gate_of)


def combine_kernel(high_far, low_far, returned, hidden_far, out_ref, mixing, hidden, sems):
    rows = hidden.shape[0]
    half = high_far.shape[0]
    copies = [
        pltpu.make_async_copy(high_far, mixing.at[pl.ds(0, half)], sems.at[0]),
        pltpu.make_async_copy(low_far, mixing.at[pl.ds(half, half)], sems.at[1]),
        pltpu.make_async_copy(hidden_far, hidden, sems.at[2]),
    ]
    for copy in copies:
        copy.start()
    for copy in copies:
        copy.wait()
    mixed = jnp.dot(mixing[...], returned[...], preferred_element_type=jnp.float32)
    mixed = mixed[:half] + mixed[half:]
    for i in range(half // rows):
        lanes = slice(i * BLOCK, (i + 1) * BLOCK)
        out_ref[:, lanes] = (hidden[:, lanes] + mixed[i * rows : (i + 1) * rows]).astype(
            jnp.bfloat16
        )


def combine(high, low, returned, hidden):
    far = [pltpu.with_memory_space_constraint(array, pltpu.HBM) for array in (high, low, hidden)]
    return pl.pallas_call(
        combine_kernel,
        out_shape=jax.ShapeDtypeStruct(hidden.shape, jnp.bfloat16),
        in_specs=[HBM, HBM, VMEM, HBM],
        out_specs=VMEM,
        scratch_shapes=[
            pltpu.VMEM((2 * high.shape[0], high.shape[1]), jnp.bfloat16),
            pltpu.VMEM(hidden.shape, jnp.float32),
            pltpu.SemaphoreType.DMA((3,)),
        ],
        compiler_params=pltpu.CompilerParams(vmem_limit_bytes=8 << 20),
        cost_estimate=pl.CostEstimate(
            flops=540_000_000, bytes_accessed=3_500_000, transcendentals=0
        ),
        name="combine",
    )(far[0], far[1], returned, far[2])


def route_gates(logits, routes):
    matches = routes[:, :, None] == jnp.arange(logits.shape[1], dtype=jnp.int32)[None, None, :]
    chosen = jnp.sum(jnp.where(matches, logits[:, None, :], 0.0), axis=-1)
    raised = jnp.exp(chosen)
    return raised / jnp.sum(raised, axis=1, keepdims=True)


def rank_of(flat_routes, experts):
    onehot = (flat_routes[:, None] == jnp.arange(experts, dtype=jnp.int32)[None, :]).astype(
        jnp.int32
    )
    earlier = jnp.cumsum(onehot, axis=0) - onehot
    return jnp.sum(earlier * onehot, axis=1)


def add(left, right):
    return (left.astype(jnp.float32) + right.astype(jnp.float32)).astype(jnp.bfloat16)


def scatter_sum(regrouped, mine, beside, spot, peers):
    jump = {"y": 1, "Y": 3, "z": 4, "Z": 12}

    def swap(array, way):
        return lax.ppermute(array, "dev", [(i, i ^ (2 * jump[way])) for i in range(peers)])

    orders = ("yYzZ", "YyzZ", "zZyY", "ZzyY")
    masks = []
    for order in orders:
        places = []
        for place in range(16):
            mask = 0
            for bit, way in enumerate(order):
                if place >> (3 - bit) & 1:
                    mask ^= jump[way]
            places.append(mask)
        masks.append(tuple(places))
    sent = project(regrouped, mine, beside, spot, [places[8:] for places in masks], "project_sent")
    got = [swap(array, order[0]) for array, order in zip(sent, orders)]
    regrouped, _ = lax.optimization_barrier((regrouped, sent[0]))
    kept = list(
        project(regrouped, mine, beside, spot, [places[:8] for places in masks], "project_kept")
    )
    for part, order in enumerate(orders):
        both = add(kept[part], got[part])
        half = both.shape[0] // 2
        kept[part], got[part] = both[:half], swap(both[half:], order[1])
    merged = []
    for pair in (0, 2):
        way, last = orders[pair][2:]
        both = jnp.concatenate(
            [add(kept[pair], got[pair]), add(kept[pair + 1], got[pair + 1])], axis=2
        )
        merged.append((both[:2], swap(both[2:], way), last))
    ends = []
    for keep, arrived, last in merged:
        both = add(keep, arrived)
        ends += [both[0], swap(both[1], last)]
    return ends


def shards(
    queries,
    new_keys,
    new_values,
    key_pages,
    value_pages,
    block_tables,
    context_lengths,
    out_weight,
    residual,
    norm_gain,
    router_weight,
    routes,
    expert_gate,
    expert_up,
    expert_down,
):
    rows, width = residual.shape
    peers = lax.axis_size("dev")
    chips = peers // 2
    place = lax.axis_index("dev")
    spot = jnp.stack([place >> 1, place & 1])
    queries, spot = lax.optimization_barrier((queries, spot))
    same_core = [[2 * chip + side for chip in range(chips)] for side in range(2)]
    experts = router_weight.shape[1]
    capacity = 2
    blocks = width // BLOCK
    lines = blocks * capacity

    weight_beside = lax.ppermute(out_weight, "dev", [(i, i ^ 1) for i in range(peers)])
    attended = attend(
        queries,
        new_keys,
        new_values,
        key_pages,
        value_pages,
        block_tables,
        context_lengths,
        chips,
    )
    regrouped = lax.all_to_all(
        attended, "dev", split_axis=0, concat_axis=0, axis_index_groups=same_core, tiled=True
    )
    routes, regrouped = lax.optimization_barrier((routes, regrouped))
    ends = scatter_sum(regrouped, out_weight, weight_beside, spot, peers)

    rank = rank_of(routes.reshape(-1), experts).reshape(rows, -1)
    block_ids = jnp.arange(blocks, dtype=jnp.int32)
    target = (routes * lines + rank)[None] + (block_ids * capacity)[:, None, None]
    target = target.reshape(blocks * rows, -1)
    line = jnp.arange(experts * lines, dtype=jnp.int32)
    placed = line[:, None] == target[:, 0][None, :]
    for k in range(1, target.shape[1]):
        placed = placed | (line[:, None] == target[:, k][None, :])
    placing = placed.astype(jnp.bfloat16)

    hidden_state, normed, sent = dispatch(*ends, residual, norm_gain[None], placing)
    arrived = lax.all_to_all(
        sent.reshape(experts, lines, BLOCK),
        ("attn", "dev"),
        split_axis=0,
        concat_axis=0,
        tiled=True,
    )
    output_rows = run_expert(arrived, expert_gate, expert_up, expert_down)
    returned = lax.all_to_all(
        output_rows, ("attn", "dev"), split_axis=0, concat_axis=0, tiled=True
    ).reshape(experts * lines, BLOCK)

    logits = jnp.dot(normed, router_weight, preferred_element_type=jnp.float32)
    gate_values = route_gates(logits, routes)
    gate_of = jnp.tile(gate_values, (blocks, 1))
    high, low = mix(target, gate_of, experts * lines)
    return combine(high, low, returned, hidden_state)


def solution(mesh):
    in_specs = (
        P(("attn", "dev"), None),
        P(("attn", "dev"), None),
        P(("attn", "dev"), None),
        P(("attn", "dev"), None, None),
        P(("attn", "dev"), None, None),
        P(("attn", "dev"), None),
        P(("attn", "dev")),
        P("dev", None),
        P(("attn", "dev"), None),
        P(),
        P(),
        P(("attn", "dev"), None),
        P(("attn", "dev"), None, None),
        P(("attn", "dev"), None, None),
        P(("attn", "dev"), None, None),
    )
    out_specs = P(("attn", "dev"), None)
    return jax.shard_map(shards, mesh=mesh, in_specs=in_specs, out_specs=out_specs, check_vma=False)
```

```python
import functools
import math

import jax
import jax.numpy as jnp
from jax import lax
from jax.experimental import pallas as pl
from jax.experimental.pallas import tpu as pltpu
from jax.sharding import PartitionSpec as P

HEADS = 64
KVH = 4
HD = 128
GROUP = HEADS // KVH
MAXCTX = 64
PAGE = 16
EPSILON = 1e-06
BLOCK = 512
ROWS = 32
CAPACITY = 2
TOGETHER = 4
CONTRACT_LAST = (((1,), (1,)), ((), ()))
VMEM = pl.BlockSpec(memory_space=pltpu.VMEM)
SMEM = pl.BlockSpec(memory_space=pltpu.SMEM)
HBM = pl.BlockSpec(memory_space=pltpu.HBM)


def attention_kernel(
    tables_far,
    lengths_far,
    q_far,
    own_key_far,
    own_value_far,
    keys_far,
    values_far,
    routes_far,
    out_far,
    target_far,
    tables,
    lengths,
    routes,
    routes_near,
    target,
    q_near,
    own_key,
    own_value,
    keys,
    values,
    q_turned,
    out_turned,
    scores_held,
    own_held,
    weights_held,
    own_weights_held,
    out_near,
    sems,
    out_sems,
):
    rows = q_near.shape[0]
    pages = MAXCTX // PAGE
    tall, wide = TOGETHER * GROUP, TOGETHER * MAXCTX
    big = tall * KVH
    scale = 1.0 / math.sqrt(HD)
    inward = [
        pltpu.make_async_copy(far, near, sems.at[i])
        for i, (far, near) in enumerate(
            (
                (q_far, q_near),
                (own_key_far, own_key),
                (keys_far, keys),
                (values_far, values),
                (own_value_far, own_value),
                (tables_far, tables),
                (lengths_far, lengths),
                (routes_far, routes),
                (routes_far, routes_near),
            )
        )
    ]
    for copy in inward[:3] + inward[5:]:
        copy.start()
    inward[7].wait()
    inward[8].wait()
    chosen = routes_near[...]
    column = lax.broadcasted_iota(jnp.int32, chosen.shape, 1)
    rank = jnp.zeros_like(chosen)
    for t in range(rows - 1):
        named = jnp.zeros_like(chosen)
        for k in range(routes.shape[0]):
            named = jnp.where(chosen == routes[k, t], 1, named)
        rank = rank + jnp.where(column > t, named, 0)
    blocks = target.shape[1] // rows
    first_line = chosen * (blocks * CAPACITY) + rank
    target[...] = jnp.concatenate(
        [first_line + block * CAPACITY for block in range(blocks)], axis=1
    )
    target_copy = pltpu.make_async_copy(target, target_far, sems.at[9])
    target_copy.start()
    inward[0].wait()
    for head in range(HEADS):
        q_turned[head // GROUP, pl.ds(head % GROUP * rows, rows), :] = q_near[
            :, head * HD : (head + 1) * HD
        ].astype(jnp.float32)
    inward[1].wait()
    inward[2].wait()
    inward[3].start()
    inward[4].start()
    inward[5].wait()
    inward[6].wait()
    for first in range(0, rows, TOGETHER):
        page_ids = [tables[j, first + i] for i in range(TOGETHER) for j in range(pages)]
        for kv in range(KVH):
            lanes = slice(kv * HD, (kv + 1) * HD)
            q = jnp.concatenate(
                [
                    q_turned[kv, pl.ds(first + i, GROUP, stride=rows), :]
                    for i in range(TOGETHER)
                ],
                axis=0,
            ).astype(jnp.bfloat16)
            k = jnp.concatenate([keys[page, :, lanes] for page in page_ids], axis=0)
            at = pl.ds(first // TOGETHER * big + kv * tall, tall)
            scores_held[at, :] = (
                lax.dot_general(q, k, CONTRACT_LAST, preferred_element_type=jnp.float32) * scale
            )
            own_held[at, :] = (
                lax.dot_general(
                    q, own_key[:, lanes], CONTRACT_LAST, preferred_element_type=jnp.float32
                )
                * scale
            )
    row_request = lax.broadcasted_iota(jnp.int32, (big, wide), 0) // GROUP % TOGETHER
    place = lax.broadcasted_iota(jnp.int32, (big, wide), 1) - row_request * MAXCTX
    own_request = lax.broadcasted_iota(jnp.int32, (big, rows), 0) // GROUP % TOGETHER
    own_column = lax.broadcasted_iota(jnp.int32, (big, rows), 1)
    for first in range(0, rows, TOGETHER):
        at = pl.ds(first // TOGETHER * big, big)
        limit = jnp.zeros((big, wide), jnp.int32)
        for i in range(TOGETHER):
            limit = jnp.where(row_request == i, lengths[first + i], limit)
        scores = jnp.where((place >= 0) & (place < limit), scores_held[at, :], -jnp.inf)
        own_score = jnp.where(own_column == own_request + first, own_held[at, :], -jnp.inf)
        top = jnp.maximum(
            jnp.max(scores, axis=1, keepdims=True), jnp.max(own_score, axis=1, keepdims=True)
        )
        weights = jnp.exp(scores - top)
        own_weights = jnp.exp(own_score - top)
        share = 1.0 / (
            jnp.sum(weights, axis=1, keepdims=True) + jnp.sum(own_weights, axis=1, keepdims=True)
        )
        weights_held[at, :] = (weights * share).astype(jnp.bfloat16)
        own_weights_held[at, :] = (own_weights * share).astype(jnp.bfloat16)
    inward[3].wait()
    inward[4].wait()
    outward = []
    held = out_near.shape[2] // HD
    span = GROUP // held
    for kv in range(KVH):
        lanes = slice(kv * HD, (kv + 1) * HD)
        for first in range(0, rows, TOGETHER):
            page_ids = [tables[j, first + i] for i in range(TOGETHER) for j in range(pages)]
            at = pl.ds(first // TOGETHER * big + kv * tall, tall)
            v = jnp.concatenate([values[page, :, lanes] for page in page_ids], axis=0)
            blended = jnp.dot(
                weights_held[at, :], v, preferred_element_type=jnp.float32
            ) + jnp.dot(
                own_weights_held[at, :], own_value[:, lanes], preferred_element_type=jnp.float32
            )
            for i in range(TOGETHER):
                out_turned[kv, pl.ds(first + i, GROUP, stride=rows), :] = blended[
                    i * GROUP : (i + 1) * GROUP
                ]
        for head in range(kv * GROUP, (kv + 1) * GROUP):
            out_near[head // held, :, head % held * HD : (head % held + 1) * HD] = out_turned[
                kv, pl.ds(head % GROUP * rows, rows), :
            ].astype(jnp.bfloat16)
        part = pl.ds(kv * span, span)
        copy = pltpu.make_async_copy(out_near.at[part], out_far.at[part], out_sems.at[kv])
        copy.start()
        outward.append(copy)
    for copy in outward:
        copy.wait()
    target_copy.wait()


def attend(
    queries, new_keys, new_values, key_pool, value_pool, tables, lengths, routes, chips, blocks
):
    rows = queries.shape[0]
    total = HEADS * rows
    shape = (chips, rows, HEADS * HD // chips)
    wide = TOGETHER * MAXCTX
    bf16, f32 = jnp.bfloat16, jnp.float32
    return pl.pallas_call(
        attention_kernel,
        out_shape=[
            pltpu.HBM(shape, bf16),
            pltpu.HBM((routes.shape[1], blocks * rows), jnp.int32),
        ],
        in_specs=[HBM] * 8,
        out_specs=[HBM] * 2,
        scratch_shapes=[
            pltpu.SMEM(tables.shape[::-1], jnp.int32),
            pltpu.SMEM(lengths.shape, jnp.int32),
            pltpu.SMEM(routes.shape[::-1], jnp.int32),
            pltpu.VMEM(routes.shape[::-1], jnp.int32),
            pltpu.VMEM((routes.shape[1], blocks * rows), jnp.int32),
            pltpu.VMEM(queries.shape, bf16),
            pltpu.VMEM(new_keys.shape, bf16),
            pltpu.VMEM(new_values.shape, bf16),
            pltpu.VMEM(key_pool.shape, bf16),
            pltpu.VMEM(value_pool.shape, bf16),
            pltpu.VMEM((KVH, GROUP * rows, HD), f32),
            pltpu.VMEM((KVH, GROUP * rows, HD), f32),
            pltpu.VMEM((total, wide), f32),
            pltpu.VMEM((total, rows), f32),
            pltpu.VMEM((total, wide), bf16),
            pltpu.VMEM((total, rows), bf16),
            pltpu.VMEM(shape, bf16),
            pltpu.SemaphoreType.DMA((10,)),
            pltpu.SemaphoreType.DMA((KVH,)),
        ],
        compiler_params=pltpu.CompilerParams(vmem_limit_bytes=12 << 20),
        cost_estimate=pl.CostEstimate(
            flops=600_000_000, bytes_accessed=5_000_000, transcendentals=300_000
        ),
        name="attention",
    )(
        *(
            pltpu.with_memory_space_constraint(array, pltpu.HBM)
            for array in (
                tables.T,
                lengths,
                queries,
                new_keys,
                new_values,
                key_pool,
                value_pool,
                routes.T,
            )
        )
    )


def projection_kernel(orders, spot, x_ref, mine, beside, *outs):
    chip, core = spot[0], spot[1]
    depth = mine.shape[0]
    columns = outs[0].shape[2]
    for i, (masks, out) in enumerate(zip(orders, outs)):
        lanes = slice(i * columns, (i + 1) * columns)
        x = jnp.concatenate([x_ref[chip ^ mask] for mask in masks], axis=0)
        low, high = x[:, :depth], x[:, depth:]
        here = jnp.full(low.shape, core, jnp.int32) == 0
        out[...] = (
            (
                jnp.dot(
                    jnp.where(here, low, high),
                    mine[:, lanes],
                    preferred_element_type=jnp.float32,
                )
                + jnp.dot(
                    jnp.where(here, high, low),
                    beside[:, lanes],
                    preferred_element_type=jnp.float32,
                )
            )
            .astype(jnp.bfloat16)
            .reshape(out.shape)
        )


def project(regrouped, mine, beside, spot, orders, name):
    _, rows, _ = regrouped.shape
    columns = mine.shape[1] // len(orders)
    return pl.pallas_call(
        functools.partial(projection_kernel, orders),
        out_shape=[
            jax.ShapeDtypeStruct((len(masks), rows, columns), jnp.bfloat16) for masks in orders
        ],
        in_specs=[SMEM, VMEM, VMEM, VMEM],
        out_specs=[VMEM] * len(orders),
        compiler_params=pltpu.CompilerParams(vmem_limit_bytes=8 << 20),
        cost_estimate=pl.CostEstimate(
            flops=540_000_000, bytes_accessed=5_500_000, transcendentals=0
        ),
        name=name,
    )(
        spot,
        regrouped,
        pltpu.with_memory_space_constraint(mine, pltpu.VMEM),
        pltpu.with_memory_space_constraint(beside, pltpu.VMEM),
    )


def dispatch_kernel(
    keep_a,
    got_a,
    keep_b,
    got_b,
    residual,
    gain,
    placing,
    hidden_far,
    normed_far,
    sent_ref,
    hidden_ref,
    normed_ref,
    sems,
):
    rows = residual.shape[0]
    halves = []
    at = 0
    for keep, got in ((keep_a, got_a), (keep_b, got_b)):
        span = keep.shape[1]
        halves.append(
            residual[:, at : at + span].astype(jnp.float32)
            + (keep[...].astype(jnp.float32) + got[...].astype(jnp.float32))
        )
        at += span
    hidden = jnp.concatenate(halves, axis=1)
    hidden_ref[...] = hidden
    mean_square = jnp.mean(hidden * hidden, axis=1, keepdims=True)
    normed = (hidden * lax.rsqrt(mean_square + EPSILON) * gain[...]).astype(jnp.bfloat16)
    normed_ref[...] = normed
    copies = [
        pltpu.make_async_copy(hidden_ref, hidden_far, sems.at[0]),
        pltpu.make_async_copy(normed_ref, normed_far, sems.at[1]),
    ]
    for copy in copies:
        copy.start()
    blocks = at // BLOCK
    stacked = jnp.concatenate(
        [normed[:, i * BLOCK : (i + 1) * BLOCK] for i in range(blocks)], axis=0
    )
    step = 512
    for i in range(0, placing.shape[0], step):
        part = pl.ds(i, step)
        sent_ref[part, :] = jnp.dot(
            placing[part, :], stacked, preferred_element_type=jnp.float32
        ).astype(jnp.bfloat16)
    for copy in copies:
        copy.wait()


def dispatch(keep_a, got_a, keep_b, got_b, residual, gain, placing):
    rows, width = residual.shape
    return pl.pallas_call(
        dispatch_kernel,
        out_shape=[
            pltpu.HBM((rows, width), jnp.float32),
            pltpu.HBM((rows, width), jnp.bfloat16),
            jax.ShapeDtypeStruct((placing.shape[0], BLOCK), jnp.bfloat16),
        ],
        in_specs=[VMEM] * 7,
        out_specs=[HBM, HBM, VMEM],
        scratch_shapes=[
            pltpu.VMEM((rows, width), jnp.float32),
            pltpu.VMEM((rows, width), jnp.bfloat16),
            pltpu.SemaphoreType.DMA((2,)),
        ],
        compiler_params=pltpu.CompilerParams(vmem_limit_bytes=8 << 20),
        cost_estimate=pl.CostEstimate(
            flops=270_000_000, bytes_accessed=4_000_000, transcendentals=16
        ),
        name="dispatch",
    )(keep_a, got_a, keep_b, got_b, residual, gain, placing)


def turning(blocks, capacity, sources, back):
    lines = blocks * capacity * sources
    left = lax.broadcasted_iota(jnp.int32, (lines, lines), 0)
    right = lax.broadcasted_iota(jnp.int32, (lines, lines), 1)
    if back:
        left, right = right, left
    wanted = left % sources * (blocks * capacity) + left // sources
    return (wanted == right).astype(jnp.float32).astype(jnp.bfloat16)


def expert_kernel(
    arrived, gate, up, down, out_far, rows_in, hidden, rows_out, out_near, sems
):
    groups = rows_out.shape[0]
    width = rows_in.shape[1]
    sources = arrived.shape[0] // groups
    blocks = width // BLOCK
    lines = arrived.shape[1] * sources
    each = lines // blocks
    capacity = arrived.shape[1] // blocks
    turn = turning(blocks, capacity, sources, False)
    for g in range(groups):
        turned = jnp.dot(
            turn,
            arrived[g * sources : (g + 1) * sources].reshape(lines, BLOCK),
            preferred_element_type=jnp.float32,
        ).astype(jnp.bfloat16)
        for i in range(blocks):
            rows_in[g * each : (g + 1) * each, i * BLOCK : (i + 1) * BLOCK] = turned[
                i * each : (i + 1) * each
            ]
    units = hidden.shape[1]
    step = 256
    for at in range(0, units, step):
        lanes = slice(at, at + step)
        gated = jnp.dot(rows_in[...], gate[0, :, lanes], preferred_element_type=jnp.float32)
        raised = jnp.dot(rows_in[...], up[0, :, lanes], preferred_element_type=jnp.float32)
        hidden[:, lanes] = (gated / (1.0 + jnp.exp(-gated)) * raised).astype(jnp.bfloat16)
    for i in range(blocks):
        lanes = slice(i * BLOCK, (i + 1) * BLOCK)
        output = jnp.dot(hidden[...], down[0, :, lanes], preferred_element_type=jnp.float32)
        rows_out[:, i * each : (i + 1) * each, :] = output.astype(jnp.bfloat16).reshape(
            groups, each, BLOCK
        )
    turn = turning(blocks, capacity, sources, True)
    outward = []
    for g in range(groups):
        part = pl.ds(g * sources, sources)
        out_near[part] = (
            jnp.dot(turn, rows_out[g], preferred_element_type=jnp.float32)
            .astype(jnp.bfloat16)
            .reshape(sources, arrived.shape[1], BLOCK)
        )
        copy = pltpu.make_async_copy(out_near.at[part], out_far.at[part], sems.at[g])
        copy.start()
        outward.append(copy)
    for copy in outward:
        copy.wait()


def run_expert(arrived, gate, up, down):
    experts, lines, _ = arrived.shape
    _, width, units = gate.shape
    token_rows = experts * lines // (width // BLOCK)
    groups = token_rows // ROWS
    return pl.pallas_call(
        expert_kernel,
        out_shape=pltpu.HBM(arrived.shape, jnp.bfloat16),
        in_specs=[VMEM] * 4,
        out_specs=HBM,
        scratch_shapes=[
            pltpu.VMEM((token_rows, width), jnp.bfloat16),
            pltpu.VMEM((token_rows, units), jnp.bfloat16),
            pltpu.VMEM((groups, token_rows, BLOCK), jnp.bfloat16),
            pltpu.VMEM(arrived.shape, jnp.bfloat16),
            pltpu.SemaphoreType.DMA((groups,)),
        ],
        compiler_params=pltpu.CompilerParams(vmem_limit_bytes=12 << 20),
        cost_estimate=pl.CostEstimate(
            flops=5_900_000_000, bytes_accessed=23_000_000, transcendentals=200_000
        ),
        name="expert",
    )(
        arrived,
        *(pltpu.with_memory_space_constraint(array, pltpu.VMEM) for array in (gate, up, down)),
    )


def mixing_kernel(target_ref, gates, mixing_far, mixing_ref, sem):
    tall, wide = mixing_ref.shape
    target = target_ref[...].T
    gate_of = jnp.concatenate([gates[...]] * (tall // gates.shape[0]), axis=0)
    step = 256
    for at in range(0, wide, step):
        line = lax.broadcasted_iota(jnp.int32, (tall, step), 1) + at
        mixing = jnp.zeros((tall, step), jnp.float32)
        for k in range(target.shape[1]):
            mixing = jnp.where(line == target[:, k : k + 1], gate_of[:, k : k + 1], mixing)
        mixing_ref[:, at : at + step] = mixing.astype(jnp.bfloat16)
    copy = pltpu.make_async_copy(mixing_ref, mixing_far, sem)
    copy.start()
    copy.wait()


def mix(target, gates, lines):
    shape = (target.shape[1], lines)
    return pl.pallas_call(
        mixing_kernel,
        out_shape=pltpu.HBM(shape, jnp.bfloat16),
        in_specs=[VMEM, VMEM],
        out_specs=HBM,
        scratch_shapes=[pltpu.VMEM(shape, jnp.bfloat16), pltpu.SemaphoreType.DMA],
        compiler_params=pltpu.CompilerParams(vmem_limit_bytes=8 << 20),
        cost_estimate=pl.CostEstimate(flops=6_000_000, bytes_accessed=600_000, transcendentals=0),
        name="mixing",
    )(target, gates)


def combine_kernel(mixing_far, returned, hidden_far, out_ref, mixing, hidden, sems):
    rows = hidden.shape[0]
    copies = [
        pltpu.make_async_copy(mixing_far, mixing, sems.at[0]),
        pltpu.make_async_copy(hidden_far, hidden, sems.at[1]),
    ]
    for copy in copies:
        copy.start()
    copies[0].wait()
    mixed = jnp.dot(mixing[...], returned[...], preferred_element_type=jnp.float32)
    copies[1].wait()
    for i in range(mixed.shape[0] // rows):
        lanes = slice(i * BLOCK, (i + 1) * BLOCK)
        out_ref[:, lanes] = (hidden[:, lanes] + mixed[i * rows : (i + 1) * rows]).astype(
            jnp.bfloat16
        )


def combine(mixing, returned, hidden):
    far = [pltpu.with_memory_space_constraint(array, pltpu.HBM) for array in (mixing, hidden)]
    return pl.pallas_call(
        combine_kernel,
        out_shape=jax.ShapeDtypeStruct(hidden.shape, jnp.bfloat16),
        in_specs=[HBM, VMEM, HBM],
        out_specs=VMEM,
        scratch_shapes=[
            pltpu.VMEM(mixing.shape, jnp.bfloat16),
            pltpu.VMEM(hidden.shape, jnp.float32),
            pltpu.SemaphoreType.DMA((2,)),
        ],
        compiler_params=pltpu.CompilerParams(vmem_limit_bytes=8 << 20),
        cost_estimate=pl.CostEstimate(
            flops=270_000_000, bytes_accessed=3_000_000, transcendentals=0
        ),
        name="combine",
    )(far[0], returned, far[1])


def route_gates(logits, routes):
    matches = routes[:, :, None] == jnp.arange(logits.shape[1], dtype=jnp.int32)[None, None, :]
    chosen = jnp.sum(jnp.where(matches, logits[:, None, :], 0.0), axis=-1)
    raised = jnp.exp(chosen)
    return raised / jnp.sum(raised, axis=1, keepdims=True)


def add(left, right):
    return (left.astype(jnp.float32) + right.astype(jnp.float32)).astype(jnp.bfloat16)


def scatter_sum(regrouped, mine, beside, spot, peers):
    jump = {"y": 1, "Y": 3, "z": 4, "Z": 12}

    def swap(array, way):
        return lax.ppermute(array, "dev", [(i, i ^ (2 * jump[way])) for i in range(peers)])

    orders = ("yYzZ", "YyzZ", "zZyY", "ZzyY")
    masks = []
    for order in orders:
        places = []
        for place in range(16):
            mask = 0
            for bit, way in enumerate(order):
                if place >> (3 - bit) & 1:
                    mask ^= jump[way]
            places.append(mask)
        masks.append(tuple(places))
    sent = project(regrouped, mine, beside, spot, [places[8:] for places in masks], "project_sent")
    got = [swap(array, order[0]) for array, order in zip(sent, orders)]
    regrouped, _ = lax.optimization_barrier((regrouped, sent[0]))
    kept = list(
        project(regrouped, mine, beside, spot, [places[:8] for places in masks], "project_kept")
    )
    for part, order in enumerate(orders):
        both = add(kept[part], got[part])
        half = both.shape[0] // 2
        kept[part], got[part] = both[:half], swap(both[half:], order[1])
    merged = []
    for pair in (0, 2):
        way, last = orders[pair][2:]
        both = jnp.concatenate(
            [add(kept[pair], got[pair]), add(kept[pair + 1], got[pair + 1])], axis=2
        )
        merged.append((both[:2], swap(both[2:], way), last))
    ends = []
    for keep, arrived, last in merged:
        both = add(keep, arrived)
        ends += [both[0], swap(both[1], last)]
    return ends


def shards(
    queries,
    new_keys,
    new_values,
    key_pages,
    value_pages,
    block_tables,
    context_lengths,
    out_weight,
    residual,
    norm_gain,
    router_weight,
    routes,
    expert_gate,
    expert_up,
    expert_down,
):
    rows, width = residual.shape
    peers = lax.axis_size("dev")
    chips = peers // 2
    place = lax.axis_index("dev")
    spot = jnp.stack([place >> 1, place & 1])
    queries, spot = lax.optimization_barrier((queries, spot))
    same_core = [[2 * chip + side for chip in range(chips)] for side in range(2)]
    experts = router_weight.shape[1]
    blocks = width // BLOCK
    lines = blocks * CAPACITY

    weight_beside = lax.ppermute(out_weight, "dev", [(i, i ^ 1) for i in range(peers)])
    attended, target = attend(
        queries,
        new_keys,
        new_values,
        key_pages,
        value_pages,
        block_tables,
        context_lengths,
        routes,
        chips,
        blocks,
    )
    regrouped = lax.all_to_all(
        attended, "dev", split_axis=0, concat_axis=0, axis_index_groups=same_core, tiled=True
    )
    ends = scatter_sum(regrouped, out_weight, weight_beside, spot, peers)

    line = jnp.arange(experts * lines, dtype=jnp.int32)
    placed = line[:, None] == target[0][None, :]
    for k in range(1, target.shape[0]):
        placed = placed | (line[:, None] == target[k][None, :])
    placing = placed.astype(jnp.bfloat16)

    hidden_state, normed, sent = dispatch(*ends, residual, norm_gain[None], placing)
    arrived = lax.all_to_all(
        sent.reshape(experts, lines, BLOCK),
        ("attn", "dev"),
        split_axis=0,
        concat_axis=0,
        tiled=True,
    )
    output_rows = run_expert(arrived, expert_gate, expert_up, expert_down)
    returned = lax.all_to_all(
        output_rows, ("attn", "dev"), split_axis=0, concat_axis=0, tiled=True
    ).reshape(experts * lines, BLOCK)

    logits = jnp.dot(normed, router_weight, preferred_element_type=jnp.float32)
    gate_values = route_gates(logits, routes)
    mixing = mix(target, gate_values, experts * lines)
    return combine(mixing, returned, hidden_state)


def solution(mesh):
    in_specs = (
        P(("attn", "dev"), None),
        P(("attn", "dev"), None),
        P(("attn", "dev"), None),
        P(("attn", "dev"), None, None),
        P(("attn", "dev"), None, None),
        P(("attn", "dev"), None),
        P(("attn", "dev")),
        P("dev", None),
        P(("attn", "dev"), None),
        P(),
        P(),
        P(("attn", "dev"), None),
        P(("attn", "dev"), None, None),
        P(("attn", "dev"), None, None),
        P(("attn", "dev"), None, None),
    )
    out_specs = P(("attn", "dev"), None)
    return jax.shard_map(shards, mesh=mesh, in_specs=in_specs, out_specs=out_specs, check_vma=False)
```

```python
import functools
import math

import jax
import jax.numpy as jnp
from jax import lax
from jax.experimental import pallas as pl
from jax.experimental.pallas import tpu as pltpu
from jax.sharding import PartitionSpec as P

HEADS = 64
KVH = 4
HD = 128
GROUP = HEADS // KVH
MAXCTX = 64
PAGE = 16
EPSILON = 1e-06
BLOCK = 512
ROWS = 32
CAPACITY = 2
TOGETHER = 4
CONTRACT_LAST = (((1,), (1,)), ((), ()))
VMEM = pl.BlockSpec(memory_space=pltpu.VMEM)
SMEM = pl.BlockSpec(memory_space=pltpu.SMEM)
HBM = pl.BlockSpec(memory_space=pltpu.HBM)


def attention_kernel(
    tables_far,
    lengths_far,
    q_far,
    own_key_far,
    own_value_far,
    keys_far,
    values_far,
    routes_far,
    out_far,
    target_far,
    tables,
    lengths,
    routes,
    routes_near,
    target,
    q_near,
    own_key,
    own_value,
    keys,
    values,
    q_turned,
    out_turned,
    scores_held,
    own_held,
    weights_held,
    own_weights_held,
    out_near,
    sems,
    out_sems,
):
    rows = q_near.shape[0]
    pages = MAXCTX // PAGE
    tall, wide = TOGETHER * GROUP, TOGETHER * MAXCTX
    big = tall * KVH
    scale = 1.0 / math.sqrt(HD)
    inward = [
        pltpu.make_async_copy(far, near, sems.at[i])
        for i, (far, near) in enumerate(
            (
                (q_far, q_near),
                (own_key_far, own_key),
                (keys_far, keys),
                (values_far, values),
                (own_value_far, own_value),
                (tables_far, tables),
                (lengths_far, lengths),
                (routes_far, routes),
                (routes_far, routes_near),
            )
        )
    ]
    for copy in inward[:3] + inward[5:]:
        copy.start()
    inward[7].wait()
    inward[8].wait()
    chosen = routes_near[...]
    column = lax.broadcasted_iota(jnp.int32, chosen.shape, 1)
    rank = jnp.zeros_like(chosen)
    for t in range(rows - 1):
        named = jnp.zeros_like(chosen)
        for k in range(routes.shape[0]):
            named = jnp.where(chosen == routes[k, t], 1, named)
        rank = rank + jnp.where(column > t, named, 0)
    blocks = target.shape[1] // rows
    first_line = chosen * (blocks * CAPACITY) + rank
    target[...] = jnp.concatenate(
        [first_line + block * CAPACITY for block in range(blocks)], axis=1
    )
    target_copy = pltpu.make_async_copy(target, target_far, sems.at[9])
    target_copy.start()
    inward[0].wait()
    for head in range(HEADS):
        q_turned[head // GROUP, pl.ds(head % GROUP * rows, rows), :] = q_near[
            :, head * HD : (head + 1) * HD
        ].astype(jnp.float32)
    inward[1].wait()
    inward[2].wait()
    inward[3].start()
    inward[4].start()
    inward[5].wait()
    inward[6].wait()
    for first in range(0, rows, TOGETHER):
        page_ids = [tables[j, first + i] for i in range(TOGETHER) for j in range(pages)]
        for kv in range(KVH):
            lanes = slice(kv * HD, (kv + 1) * HD)
            q = jnp.concatenate(
                [
                    q_turned[kv, pl.ds(first + i, GROUP, stride=rows), :]
                    for i in range(TOGETHER)
                ],
                axis=0,
            ).astype(jnp.bfloat16)
            k = jnp.concatenate([keys[page, :, lanes] for page in page_ids], axis=0)
            at = pl.ds(first // TOGETHER * big + kv * tall, tall)
            scores_held[at, :] = (
                lax.dot_general(q, k, CONTRACT_LAST, preferred_element_type=jnp.float32) * scale
            )
            own_held[at, :] = (
                lax.dot_general(
                    q, own_key[:, lanes], CONTRACT_LAST, preferred_element_type=jnp.float32
                )
                * scale
            )
    row_request = lax.broadcasted_iota(jnp.int32, (big, wide), 0) // GROUP % TOGETHER
    place = lax.broadcasted_iota(jnp.int32, (big, wide), 1) - row_request * MAXCTX
    own_request = lax.broadcasted_iota(jnp.int32, (big, rows), 0) // GROUP % TOGETHER
    own_column = lax.broadcasted_iota(jnp.int32, (big, rows), 1)
    for first in range(0, rows, TOGETHER):
        at = pl.ds(first // TOGETHER * big, big)
        limit = jnp.zeros((big, wide), jnp.int32)
        for i in range(TOGETHER):
            limit = jnp.where(row_request == i, lengths[first + i], limit)
        scores = jnp.where((place >= 0) & (place < limit), scores_held[at, :], -jnp.inf)
        own_score = jnp.where(own_column == own_request + first, own_held[at, :], -jnp.inf)
        top = jnp.maximum(
            jnp.max(scores, axis=1, keepdims=True), jnp.max(own_score, axis=1, keepdims=True)
        )
        weights = jnp.exp(scores - top)
        own_weights = jnp.exp(own_score - top)
        share = 1.0 / (
            jnp.sum(weights, axis=1, keepdims=True) + jnp.sum(own_weights, axis=1, keepdims=True)
        )
        weights_held[at, :] = (weights * share).astype(jnp.bfloat16)
        own_weights_held[at, :] = (own_weights * share).astype(jnp.bfloat16)
    inward[3].wait()
    inward[4].wait()
    outward = []
    held = out_near.shape[2] // HD
    span = GROUP // held
    for kv in range(KVH):
        lanes = slice(kv * HD, (kv + 1) * HD)
        for first in range(0, rows, TOGETHER):
            page_ids = [tables[j, first + i] for i in range(TOGETHER) for j in range(pages)]
            at = pl.ds(first // TOGETHER * big + kv * tall, tall)
            v = jnp.concatenate([values[page, :, lanes] for page in page_ids], axis=0)
            blended = jnp.dot(
                weights_held[at, :], v, preferred_element_type=jnp.float32
            ) + jnp.dot(
                own_weights_held[at, :], own_value[:, lanes], preferred_element_type=jnp.float32
            )
            for i in range(TOGETHER):
                out_turned[kv, pl.ds(first + i, GROUP, stride=rows), :] = blended[
                    i * GROUP : (i + 1) * GROUP
                ]
        for head in range(kv * GROUP, (kv + 1) * GROUP):
            out_near[head // held, :, head % held * HD : (head % held + 1) * HD] = out_turned[
                kv, pl.ds(head % GROUP * rows, rows), :
            ].astype(jnp.bfloat16)
        part = pl.ds(kv * span, span)
        copy = pltpu.make_async_copy(out_near.at[part], out_far.at[part], out_sems.at[kv])
        copy.start()
        outward.append(copy)
    for copy in outward:
        copy.wait()
    target_copy.wait()


def attend(
    queries, new_keys, new_values, key_pool, value_pool, tables, lengths, routes, chips, blocks
):
    rows = queries.shape[0]
    total = HEADS * rows
    shape = (chips, rows, HEADS * HD // chips)
    wide = TOGETHER * MAXCTX
    bf16, f32 = jnp.bfloat16, jnp.float32
    return pl.pallas_call(
        attention_kernel,
        out_shape=[
            pltpu.HBM(shape, bf16),
            pltpu.HBM((routes.shape[1], blocks * rows), jnp.int32),
        ],
        in_specs=[HBM] * 8,
        out_specs=[HBM] * 2,
        scratch_shapes=[
            pltpu.SMEM(tables.shape[::-1], jnp.int32),
            pltpu.SMEM(lengths.shape, jnp.int32),
            pltpu.SMEM(routes.shape[::-1], jnp.int32),
            pltpu.VMEM(routes.shape[::-1], jnp.int32),
            pltpu.VMEM((routes.shape[1], blocks * rows), jnp.int32),
            pltpu.VMEM(queries.shape, bf16),
            pltpu.VMEM(new_keys.shape, bf16),
            pltpu.VMEM(new_values.shape, bf16),
            pltpu.VMEM(key_pool.shape, bf16),
            pltpu.VMEM(value_pool.shape, bf16),
            pltpu.VMEM((KVH, GROUP * rows, HD), f32),
            pltpu.VMEM((KVH, GROUP * rows, HD), f32),
            pltpu.VMEM((total, wide), f32),
            pltpu.VMEM((total, rows), f32),
            pltpu.VMEM((total, wide), bf16),
            pltpu.VMEM((total, rows), bf16),
            pltpu.VMEM(shape, bf16),
            pltpu.SemaphoreType.DMA((10,)),
            pltpu.SemaphoreType.DMA((KVH,)),
        ],
        compiler_params=pltpu.CompilerParams(vmem_limit_bytes=12 << 20),
        cost_estimate=pl.CostEstimate(
            flops=600_000_000, bytes_accessed=5_000_000, transcendentals=300_000
        ),
        name="attention",
    )(
        *(
            pltpu.with_memory_space_constraint(array, pltpu.HBM)
            for array in (
                tables.T,
                lengths,
                queries,
                new_keys,
                new_values,
                key_pool,
                value_pool,
                routes.T,
            )
        )
    )


def projection_kernel(orders, spot, x_ref, mine, beside, *outs):
    chip, core = spot[0], spot[1]
    depth = mine.shape[0]
    columns = outs[0].shape[2]
    for i, (masks, out) in enumerate(zip(orders, outs)):
        lanes = slice(i * columns, (i + 1) * columns)
        x = jnp.concatenate([x_ref[chip ^ mask] for mask in masks], axis=0)
        low, high = x[:, :depth], x[:, depth:]
        here = jnp.full(low.shape, core, jnp.int32) == 0
        out[...] = (
            (
                jnp.dot(
                    jnp.where(here, low, high),
                    mine[:, lanes],
                    preferred_element_type=jnp.float32,
                )
                + jnp.dot(
                    jnp.where(here, high, low),
                    beside[:, lanes],
                    preferred_element_type=jnp.float32,
                )
            )
            .astype(jnp.bfloat16)
            .reshape(out.shape)
        )


def project(regrouped, mine, beside, spot, orders, name):
    _, rows, _ = regrouped.shape
    columns = mine.shape[1] // len(orders)
    return pl.pallas_call(
        functools.partial(projection_kernel, orders),
        out_shape=[
            jax.ShapeDtypeStruct((len(masks), rows, columns), jnp.bfloat16) for masks in orders
        ],
        in_specs=[SMEM, VMEM, VMEM, VMEM],
        out_specs=[VMEM] * len(orders),
        compiler_params=pltpu.CompilerParams(vmem_limit_bytes=8 << 20),
        cost_estimate=pl.CostEstimate(
            flops=540_000_000, bytes_accessed=5_500_000, transcendentals=0
        ),
        name=name,
    )(
        spot,
        regrouped,
        pltpu.with_memory_space_constraint(mine, pltpu.VMEM),
        pltpu.with_memory_space_constraint(beside, pltpu.VMEM),
    )


def dispatch_kernel(
    keep_a,
    got_a,
    keep_b,
    got_b,
    residual,
    gain,
    placing,
    hidden_far,
    normed_far,
    sent_ref,
    hidden_ref,
    normed_ref,
    sems,
):
    rows = residual.shape[0]
    halves = []
    at = 0
    for keep, got in ((keep_a, got_a), (keep_b, got_b)):
        span = keep.shape[1]
        halves.append(
            residual[:, at : at + span].astype(jnp.float32)
            + (keep[...].astype(jnp.float32) + got[...].astype(jnp.float32))
        )
        at += span
    hidden = jnp.concatenate(halves, axis=1)
    hidden_ref[...] = hidden
    mean_square = jnp.mean(hidden * hidden, axis=1, keepdims=True)
    normed = (hidden * lax.rsqrt(mean_square + EPSILON) * gain[...]).astype(jnp.bfloat16)
    normed_ref[...] = normed
    copies = [
        pltpu.make_async_copy(hidden_ref, hidden_far, sems.at[0]),
        pltpu.make_async_copy(normed_ref, normed_far, sems.at[1]),
    ]
    for copy in copies:
        copy.start()
    blocks = at // BLOCK
    stacked = jnp.concatenate(
        [normed[:, i * BLOCK : (i + 1) * BLOCK] for i in range(blocks)], axis=0
    )
    step = 512
    for i in range(0, placing.shape[0], step):
        part = pl.ds(i, step)
        sent_ref[part, :] = jnp.dot(
            placing[part, :], stacked, preferred_element_type=jnp.float32
        ).astype(jnp.bfloat16)
    for copy in copies:
        copy.wait()


def dispatch(keep_a, got_a, keep_b, got_b, residual, gain, placing):
    rows, width = residual.shape
    return pl.pallas_call(
        dispatch_kernel,
        out_shape=[
            pltpu.HBM((rows, width), jnp.float32),
            pltpu.HBM((rows, width), jnp.bfloat16),
            jax.ShapeDtypeStruct((placing.shape[0], BLOCK), jnp.bfloat16),
        ],
        in_specs=[VMEM] * 7,
        out_specs=[HBM, HBM, VMEM],
        scratch_shapes=[
            pltpu.VMEM((rows, width), jnp.float32),
            pltpu.VMEM((rows, width), jnp.bfloat16),
            pltpu.SemaphoreType.DMA((2,)),
        ],
        compiler_params=pltpu.CompilerParams(vmem_limit_bytes=8 << 20),
        cost_estimate=pl.CostEstimate(
            flops=270_000_000, bytes_accessed=4_000_000, transcendentals=16
        ),
        name="dispatch",
    )(keep_a, got_a, keep_b, got_b, residual, gain, placing)


def turning(blocks, capacity, sources, back):
    lines = blocks * capacity * sources
    left = lax.broadcasted_iota(jnp.int32, (lines, lines), 0)
    right = lax.broadcasted_iota(jnp.int32, (lines, lines), 1)
    if back:
        left, right = right, left
    wanted = left % sources * (blocks * capacity) + left // sources
    return (wanted == right).astype(jnp.float32).astype(jnp.bfloat16)


def expert_kernel(
    arrived, gate, up, down, out_far, rows_in, hidden, rows_out, out_near, sems
):
    groups = rows_out.shape[0]
    width = rows_in.shape[1]
    sources = arrived.shape[0] // groups
    blocks = width // BLOCK
    lines = arrived.shape[1] * sources
    each = lines // blocks
    capacity = arrived.shape[1] // blocks
    turn = turning(blocks, capacity, sources, False)
    for g in range(groups):
        turned = jnp.dot(
            turn,
            arrived[g * sources : (g + 1) * sources].reshape(lines, BLOCK),
            preferred_element_type=jnp.float32,
        ).astype(jnp.bfloat16)
        for i in range(blocks):
            rows_in[g * each : (g + 1) * each, i * BLOCK : (i + 1) * BLOCK] = turned[
                i * each : (i + 1) * each
            ]
    units = hidden.shape[1]
    step = 256
    for at in range(0, units, step):
        lanes = slice(at, at + step)
        gated = jnp.dot(rows_in[...], gate[0, :, lanes], preferred_element_type=jnp.float32)
        raised = jnp.dot(rows_in[...], up[0, :, lanes], preferred_element_type=jnp.float32)
        hidden[:, lanes] = (gated / (1.0 + jnp.exp(-gated)) * raised).astype(jnp.bfloat16)
    for i in range(blocks):
        lanes = slice(i * BLOCK, (i + 1) * BLOCK)
        output = jnp.dot(hidden[...], down[0, :, lanes], preferred_element_type=jnp.float32)
        rows_out[:, i * each : (i + 1) * each, :] = output.astype(jnp.bfloat16).reshape(
            groups, each, BLOCK
        )
    turn = turning(blocks, capacity, sources, True)
    outward = []
    for g in range(groups):
        part = pl.ds(g * sources, sources)
        out_near[part] = (
            jnp.dot(turn, rows_out[g], preferred_element_type=jnp.float32)
            .astype(jnp.bfloat16)
            .reshape(sources, arrived.shape[1], BLOCK)
        )
        copy = pltpu.make_async_copy(out_near.at[part], out_far.at[part], sems.at[g])
        copy.start()
        outward.append(copy)
    for copy in outward:
        copy.wait()


def run_expert(arrived, gate, up, down):
    experts, lines, _ = arrived.shape
    _, width, units = gate.shape
    token_rows = experts * lines // (width // BLOCK)
    groups = token_rows // ROWS
    return pl.pallas_call(
        expert_kernel,
        out_shape=pltpu.HBM(arrived.shape, jnp.bfloat16),
        in_specs=[VMEM] * 4,
        out_specs=HBM,
        scratch_shapes=[
            pltpu.VMEM((token_rows, width), jnp.bfloat16),
            pltpu.VMEM((token_rows, units), jnp.bfloat16),
            pltpu.VMEM((groups, token_rows, BLOCK), jnp.bfloat16),
            pltpu.VMEM(arrived.shape, jnp.bfloat16),
            pltpu.SemaphoreType.DMA((groups,)),
        ],
        compiler_params=pltpu.CompilerParams(vmem_limit_bytes=12 << 20),
        cost_estimate=pl.CostEstimate(
            flops=5_900_000_000, bytes_accessed=23_000_000, transcendentals=200_000
        ),
        name="expert",
    )(
        arrived,
        *(pltpu.with_memory_space_constraint(array, pltpu.VMEM) for array in (gate, up, down)),
    )


def mixing_kernel(target_ref, gates, mixing_far, mixing_ref, sem):
    tall, wide = mixing_ref.shape
    target = target_ref[...].T
    gate_of = jnp.concatenate([gates[...]] * (tall // gates.shape[0]), axis=0)
    step = 256
    for at in range(0, wide, step):
        line = lax.broadcasted_iota(jnp.int32, (tall, step), 1) + at
        mixing = jnp.zeros((tall, step), jnp.float32)
        for k in range(target.shape[1]):
            mixing = jnp.where(line == target[:, k : k + 1], gate_of[:, k : k + 1], mixing)
        mixing_ref[:, at : at + step] = mixing.astype(jnp.bfloat16)
    copy = pltpu.make_async_copy(mixing_ref, mixing_far, sem)
    copy.start()
    copy.wait()


def mix(target, gates, lines):
    shape = (target.shape[1], lines)
    return pl.pallas_call(
        mixing_kernel,
        out_shape=pltpu.HBM(shape, jnp.bfloat16),
        in_specs=[VMEM, VMEM],
        out_specs=HBM,
        scratch_shapes=[pltpu.VMEM(shape, jnp.bfloat16), pltpu.SemaphoreType.DMA],
        compiler_params=pltpu.CompilerParams(vmem_limit_bytes=8 << 20),
        cost_estimate=pl.CostEstimate(flops=6_000_000, bytes_accessed=600_000, transcendentals=0),
        name="mixing",
    )(target, gates)


def combine_kernel(mixing_far, returned, hidden_far, out_ref, mixing, hidden, sems):
    rows = hidden.shape[0]
    copies = [
        pltpu.make_async_copy(mixing_far, mixing, sems.at[0]),
        pltpu.make_async_copy(hidden_far, hidden, sems.at[1]),
    ]
    for copy in copies:
        copy.start()
    copies[0].wait()
    mixed = jnp.dot(mixing[...], returned[...], preferred_element_type=jnp.float32)
    copies[1].wait()
    for i in range(mixed.shape[0] // rows):
        lanes = slice(i * BLOCK, (i + 1) * BLOCK)
        out_ref[:, lanes] = (hidden[:, lanes] + mixed[i * rows : (i + 1) * rows]).astype(
            jnp.bfloat16
        )


def combine(mixing, returned, hidden):
    far = [pltpu.with_memory_space_constraint(array, pltpu.HBM) for array in (mixing, hidden)]
    return pl.pallas_call(
        combine_kernel,
        out_shape=jax.ShapeDtypeStruct(hidden.shape, jnp.bfloat16),
        in_specs=[HBM, VMEM, HBM],
        out_specs=VMEM,
        scratch_shapes=[
            pltpu.VMEM(mixing.shape, jnp.bfloat16),
            pltpu.VMEM(hidden.shape, jnp.float32),
            pltpu.SemaphoreType.DMA((2,)),
        ],
        compiler_params=pltpu.CompilerParams(vmem_limit_bytes=8 << 20),
        cost_estimate=pl.CostEstimate(
            flops=270_000_000, bytes_accessed=3_000_000, transcendentals=0
        ),
        name="combine",
    )(far[0], returned, far[1])


def route_gates(logits, routes):
    matches = routes[:, :, None] == jnp.arange(logits.shape[1], dtype=jnp.int32)[None, None, :]
    chosen = jnp.sum(jnp.where(matches, logits[:, None, :], 0.0), axis=-1)
    raised = jnp.exp(chosen)
    return raised / jnp.sum(raised, axis=1, keepdims=True)


def add(left, right):
    return (left.astype(jnp.float32) + right.astype(jnp.float32)).astype(jnp.bfloat16)


def scatter_sum(regrouped, mine, beside, spot, peers):
    jump = {"y": 1, "Y": 3, "z": 4, "Z": 12}

    def swap(array, way):
        return lax.ppermute(array, "dev", [(i, i ^ (2 * jump[way])) for i in range(peers)])

    orders = ("yYzZ", "YyzZ", "zZyY", "ZzyY")
    masks = []
    for order in orders:
        places = []
        for place in range(16):
            mask = 0
            for bit, way in enumerate(order):
                if place >> (3 - bit) & 1:
                    mask ^= jump[way]
            places.append(mask)
        masks.append(tuple(places))
    sent = project(regrouped, mine, beside, spot, [places[8:] for places in masks], "project_sent")
    got = [swap(array, order[0]) for array, order in zip(sent, orders)]
    regrouped, _ = lax.optimization_barrier((regrouped, sent[0]))
    kept = list(
        project(regrouped, mine, beside, spot, [places[:8] for places in masks], "project_kept")
    )
    for part, order in enumerate(orders):
        both = add(kept[part], got[part])
        half = both.shape[0] // 2
        kept[part], got[part] = both[:half], swap(both[half:], order[1])
    merged = []
    for pair in (0, 2):
        way, last = orders[pair][2:]
        both = jnp.concatenate(
            [add(kept[pair], got[pair]), add(kept[pair + 1], got[pair + 1])], axis=2
        )
        merged.append((both[:2], swap(both[2:], way), last))
    ends = []
    for keep, arrived, last in merged:
        both = add(keep, arrived)
        ends += [both[0], swap(both[1], last)]
    return ends


def shards(
    queries,
    new_keys,
    new_values,
    key_pages,
    value_pages,
    block_tables,
    context_lengths,
    out_weight,
    residual,
    norm_gain,
    router_weight,
    routes,
    expert_gate,
    expert_up,
    expert_down,
):
    rows, width = residual.shape
    peers = lax.axis_size("dev")
    chips = peers // 2
    place = lax.axis_index("dev")
    spot = jnp.stack([place >> 1, place & 1])
    queries, spot = lax.optimization_barrier((queries, spot))
    same_core = [[2 * chip + side for chip in range(chips)] for side in range(2)]
    experts = router_weight.shape[1]
    blocks = width // BLOCK
    lines = blocks * CAPACITY

    attended, target = attend(
        queries,
        new_keys,
        new_values,
        key_pages,
        value_pages,
        block_tables,
        context_lengths,
        routes,
        chips,
        blocks,
    )
    attended, weight_sent = lax.optimization_barrier((attended, out_weight))
    weight_beside = lax.ppermute(weight_sent, "dev", [(i, i ^ 1) for i in range(peers)])
    regrouped = lax.all_to_all(
        attended, "dev", split_axis=0, concat_axis=0, axis_index_groups=same_core, tiled=True
    )
    ends = scatter_sum(regrouped, out_weight, weight_beside, spot, peers)

    line = jnp.arange(experts * lines, dtype=jnp.int32)
    placed = line[:, None] == target[0][None, :]
    for k in range(1, target.shape[0]):
        placed = placed | (line[:, None] == target[k][None, :])
    placing = placed.astype(jnp.bfloat16)

    hidden_state, normed, sent = dispatch(*ends, residual, norm_gain[None], placing)
    arrived = lax.all_to_all(
        sent.reshape(experts, lines, BLOCK),
        ("attn", "dev"),
        split_axis=0,
        concat_axis=0,
        tiled=True,
    )
    output_rows = run_expert(arrived, expert_gate, expert_up, expert_down)
    returned = lax.all_to_all(
        output_rows, ("attn", "dev"), split_axis=0, concat_axis=0, tiled=True
    ).reshape(experts * lines, BLOCK)

    logits = jnp.dot(normed, router_weight, preferred_element_type=jnp.float32)
    gate_values = route_gates(logits, routes)
    mixing = mix(target, gate_values, experts * lines)
    return combine(mixing, returned, hidden_state)


def solution(mesh):
    in_specs = (
        P(("attn", "dev"), None),
        P(("attn", "dev"), None),
        P(("attn", "dev"), None),
        P(("attn", "dev"), None, None),
        P(("attn", "dev"), None, None),
        P(("attn", "dev"), None),
        P(("attn", "dev")),
        P("dev", None),
        P(("attn", "dev"), None),
        P(),
        P(),
        P(("attn", "dev"), None),
        P(("attn", "dev"), None, None),
        P(("attn", "dev"), None, None),
        P(("attn", "dev"), None, None),
    )
    out_specs = P(("attn", "dev"), None)
    return jax.shard_map(shards, mesh=mesh, in_specs=in_specs, out_specs=out_specs, check_vma=False)
```

```python
import functools
import math

import jax
import jax.numpy as jnp
from jax import lax
from jax.experimental import pallas as pl
from jax.experimental.pallas import tpu as pltpu
from jax.sharding import PartitionSpec as P

HEADS = 64
KVH = 4
HD = 128
GROUP = HEADS // KVH
MAXCTX = 64
PAGE = 16
EPSILON = 1e-06
BLOCK = 512
ROWS = 32
CAPACITY = 2
TOGETHER = 4
CONTRACT_LAST = (((1,), (1,)), ((), ()))
VMEM = pl.BlockSpec(memory_space=pltpu.VMEM)
SMEM = pl.BlockSpec(memory_space=pltpu.SMEM)
HBM = pl.BlockSpec(memory_space=pltpu.HBM)


def attention_kernel(
    tables_far,
    lengths_far,
    q_far,
    own_key_far,
    own_value_far,
    keys_far,
    values_far,
    routes_far,
    out_far,
    target_far,
    tables,
    lengths,
    routes,
    routes_near,
    target,
    q_near,
    own_key,
    own_value,
    keys,
    values,
    q_turned,
    out_turned,
    scores_held,
    own_held,
    weights_held,
    own_weights_held,
    out_near,
    sems,
    out_sems,
):
    rows = q_near.shape[0]
    pages = MAXCTX // PAGE
    tall, wide = TOGETHER * GROUP, TOGETHER * MAXCTX
    big = tall * KVH
    scale = 1.0 / math.sqrt(HD)
    inward = [
        pltpu.make_async_copy(far, near, sems.at[i])
        for i, (far, near) in enumerate(
            (
                (q_far, q_near),
                (own_key_far, own_key),
                (keys_far, keys),
                (values_far, values),
                (own_value_far, own_value),
                (tables_far, tables),
                (lengths_far, lengths),
                (routes_far, routes),
                (routes_far, routes_near),
            )
        )
    ]
    for copy in inward[:3] + inward[5:]:
        copy.start()
    inward[0].wait()
    for head in range(HEADS):
        q_turned[head // GROUP, pl.ds(head % GROUP * rows, rows), :] = q_near[
            :, head * HD : (head + 1) * HD
        ].astype(jnp.float32)
    inward[1].wait()
    inward[2].wait()
    inward[3].start()
    inward[4].start()
    inward[5].wait()
    inward[6].wait()
    for first in range(0, rows, TOGETHER):
        page_ids = [tables[j, first + i] for i in range(TOGETHER) for j in range(pages)]
        for kv in range(KVH):
            lanes = slice(kv * HD, (kv + 1) * HD)
            q = jnp.concatenate(
                [
                    q_turned[kv, pl.ds(first + i, GROUP, stride=rows), :]
                    for i in range(TOGETHER)
                ],
                axis=0,
            ).astype(jnp.bfloat16)
            k = jnp.concatenate([keys[page, :, lanes] for page in page_ids], axis=0)
            at = pl.ds(first // TOGETHER * big + kv * tall, tall)
            scores_held[at, :] = (
                lax.dot_general(q, k, CONTRACT_LAST, preferred_element_type=jnp.float32) * scale
            )
            own_held[at, :] = (
                lax.dot_general(
                    q, own_key[:, lanes], CONTRACT_LAST, preferred_element_type=jnp.float32
                )
                * scale
            )
    row_request = lax.broadcasted_iota(jnp.int32, (big, wide), 0) // GROUP % TOGETHER
    place = lax.broadcasted_iota(jnp.int32, (big, wide), 1) - row_request * MAXCTX
    own_request = lax.broadcasted_iota(jnp.int32, (big, rows), 0) // GROUP % TOGETHER
    own_column = lax.broadcasted_iota(jnp.int32, (big, rows), 1)
    for first in range(0, rows, TOGETHER):
        at = pl.ds(first // TOGETHER * big, big)
        limit = jnp.zeros((big, wide), jnp.int32)
        for i in range(TOGETHER):
            limit = jnp.where(row_request == i, lengths[first + i], limit)
        scores = jnp.where((place >= 0) & (place < limit), scores_held[at, :], -jnp.inf)
        own_score = jnp.where(own_column == own_request + first, own_held[at, :], -jnp.inf)
        top = jnp.maximum(
            jnp.max(scores, axis=1, keepdims=True), jnp.max(own_score, axis=1, keepdims=True)
        )
        weights = jnp.exp(scores - top)
        own_weights = jnp.exp(own_score - top)
        share = 1.0 / (
            jnp.sum(weights, axis=1, keepdims=True) + jnp.sum(own_weights, axis=1, keepdims=True)
        )
        weights_held[at, :] = (weights * share).astype(jnp.bfloat16)
        own_weights_held[at, :] = (own_weights * share).astype(jnp.bfloat16)
    inward[7].wait()
    inward[8].wait()
    chosen = routes_near[...]
    column = lax.broadcasted_iota(jnp.int32, chosen.shape, 1)
    rank = jnp.zeros_like(chosen)
    for t in range(rows - 1):
        named = jnp.zeros_like(chosen)
        for k in range(routes.shape[0]):
            named = jnp.where(chosen == routes[k, t], 1, named)
        rank = rank + jnp.where(column > t, named, 0)
    blocks = target.shape[1] // rows
    first_line = chosen * (blocks * CAPACITY) + rank
    target[...] = jnp.concatenate(
        [first_line + block * CAPACITY for block in range(blocks)], axis=1
    )
    target_copy = pltpu.make_async_copy(target, target_far, sems.at[9])
    target_copy.start()
    inward[3].wait()
    inward[4].wait()
    outward = []
    held = out_near.shape[2] // HD
    span = GROUP // held
    for kv in range(KVH):
        lanes = slice(kv * HD, (kv + 1) * HD)
        for first in range(0, rows, TOGETHER):
            page_ids = [tables[j, first + i] for i in range(TOGETHER) for j in range(pages)]
            at = pl.ds(first // TOGETHER * big + kv * tall, tall)
            v = jnp.concatenate([values[page, :, lanes] for page in page_ids], axis=0)
            blended = jnp.dot(
                weights_held[at, :], v, preferred_element_type=jnp.float32
            ) + jnp.dot(
                own_weights_held[at, :], own_value[:, lanes], preferred_element_type=jnp.float32
            )
            for i in range(TOGETHER):
                out_turned[kv, pl.ds(first + i, GROUP, stride=rows), :] = blended[
                    i * GROUP : (i + 1) * GROUP
                ]
        for head in range(kv * GROUP, (kv + 1) * GROUP):
            out_near[head // held, :, head % held * HD : (head % held + 1) * HD] = out_turned[
                kv, pl.ds(head % GROUP * rows, rows), :
            ].astype(jnp.bfloat16)
        part = pl.ds(kv * span, span)
        copy = pltpu.make_async_copy(out_near.at[part], out_far.at[part], out_sems.at[kv])
        copy.start()
        outward.append(copy)
    for copy in outward:
        copy.wait()
    target_copy.wait()


def attend(
    queries, new_keys, new_values, key_pool, value_pool, tables, lengths, routes, chips, blocks
):
    rows = queries.shape[0]
    total = HEADS * rows
    shape = (chips, rows, HEADS * HD // chips)
    wide = TOGETHER * MAXCTX
    bf16, f32 = jnp.bfloat16, jnp.float32
    return pl.pallas_call(
        attention_kernel,
        out_shape=[
            pltpu.HBM(shape, bf16),
            pltpu.HBM((routes.shape[1], blocks * rows), jnp.int32),
        ],
        in_specs=[HBM] * 8,
        out_specs=[HBM] * 2,
        scratch_shapes=[
            pltpu.SMEM(tables.shape[::-1], jnp.int32),
            pltpu.SMEM(lengths.shape, jnp.int32),
            pltpu.SMEM(routes.shape[::-1], jnp.int32),
            pltpu.VMEM(routes.shape[::-1], jnp.int32),
            pltpu.VMEM((routes.shape[1], blocks * rows), jnp.int32),
            pltpu.VMEM(queries.shape, bf16),
            pltpu.VMEM(new_keys.shape, bf16),
            pltpu.VMEM(new_values.shape, bf16),
            pltpu.VMEM(key_pool.shape, bf16),
            pltpu.VMEM(value_pool.shape, bf16),
            pltpu.VMEM((KVH, GROUP * rows, HD), f32),
            pltpu.VMEM((KVH, GROUP * rows, HD), f32),
            pltpu.VMEM((total, wide), f32),
            pltpu.VMEM((total, rows), f32),
            pltpu.VMEM((total, wide), bf16),
            pltpu.VMEM((total, rows), bf16),
            pltpu.VMEM(shape, bf16),
            pltpu.SemaphoreType.DMA((10,)),
            pltpu.SemaphoreType.DMA((KVH,)),
        ],
        compiler_params=pltpu.CompilerParams(vmem_limit_bytes=12 << 20),
        cost_estimate=pl.CostEstimate(
            flops=600_000_000, bytes_accessed=5_000_000, transcendentals=300_000
        ),
        name="attention",
    )(
        *(
            pltpu.with_memory_space_constraint(array, pltpu.HBM)
            for array in (
                tables.T,
                lengths,
                queries,
                new_keys,
                new_values,
                key_pool,
                value_pool,
                routes.T,
            )
        )
    )


def projection_kernel(orders, spot, x_ref, mine, beside, *outs):
    chip, core = spot[0], spot[1]
    depth = mine.shape[0]
    columns = outs[0].shape[2]
    for i, (masks, out) in enumerate(zip(orders, outs)):
        lanes = slice(i * columns, (i + 1) * columns)
        x = jnp.concatenate([x_ref[chip ^ mask] for mask in masks], axis=0)
        low, high = x[:, :depth], x[:, depth:]
        here = jnp.full(low.shape, core, jnp.int32) == 0
        out[...] = (
            (
                jnp.dot(
                    jnp.where(here, low, high),
                    mine[:, lanes],
                    preferred_element_type=jnp.float32,
                )
                + jnp.dot(
                    jnp.where(here, high, low),
                    beside[:, lanes],
                    preferred_element_type=jnp.float32,
                )
            )
            .astype(jnp.bfloat16)
            .reshape(out.shape)
        )


def project(regrouped, mine, beside, spot, orders, name):
    _, rows, _ = regrouped.shape
    columns = mine.shape[1] // len(orders)
    return pl.pallas_call(
        functools.partial(projection_kernel, orders),
        out_shape=[
            jax.ShapeDtypeStruct((len(masks), rows, columns), jnp.bfloat16) for masks in orders
        ],
        in_specs=[SMEM, VMEM, VMEM, VMEM],
        out_specs=[VMEM] * len(orders),
        compiler_params=pltpu.CompilerParams(vmem_limit_bytes=8 << 20),
        cost_estimate=pl.CostEstimate(
            flops=540_000_000, bytes_accessed=5_500_000, transcendentals=0
        ),
        name=name,
    )(
        spot,
        regrouped,
        pltpu.with_memory_space_constraint(mine, pltpu.VMEM),
        pltpu.with_memory_space_constraint(beside, pltpu.VMEM),
    )


def dispatch_kernel(
    keep_a,
    got_a,
    keep_b,
    got_b,
    residual,
    gain,
    placing,
    hidden_far,
    normed_far,
    sent_ref,
    hidden_ref,
    normed_ref,
    sems,
):
    rows = residual.shape[0]
    halves = []
    at = 0
    for keep, got in ((keep_a, got_a), (keep_b, got_b)):
        span = keep.shape[1]
        halves.append(
            residual[:, at : at + span].astype(jnp.float32)
            + (keep[...].astype(jnp.float32) + got[...].astype(jnp.float32))
        )
        at += span
    hidden = jnp.concatenate(halves, axis=1)
    hidden_ref[...] = hidden
    mean_square = jnp.mean(hidden * hidden, axis=1, keepdims=True)
    normed = (hidden * lax.rsqrt(mean_square + EPSILON) * gain[...]).astype(jnp.bfloat16)
    normed_ref[...] = normed
    copies = [
        pltpu.make_async_copy(hidden_ref, hidden_far, sems.at[0]),
        pltpu.make_async_copy(normed_ref, normed_far, sems.at[1]),
    ]
    for copy in copies:
        copy.start()
    blocks = at // BLOCK
    stacked = jnp.concatenate(
        [normed[:, i * BLOCK : (i + 1) * BLOCK] for i in range(blocks)], axis=0
    )
    step = 512
    for i in range(0, placing.shape[0], step):
        part = pl.ds(i, step)
        sent_ref[part, :] = jnp.dot(
            placing[part, :], stacked, preferred_element_type=jnp.float32
        ).astype(jnp.bfloat16)
    for copy in copies:
        copy.wait()


def dispatch(keep_a, got_a, keep_b, got_b, residual, gain, placing):
    rows, width = residual.shape
    return pl.pallas_call(
        dispatch_kernel,
        out_shape=[
            pltpu.HBM((rows, width), jnp.float32),
            pltpu.HBM((rows, width), jnp.bfloat16),
            jax.ShapeDtypeStruct((placing.shape[0], BLOCK), jnp.bfloat16),
        ],
        in_specs=[VMEM] * 7,
        out_specs=[HBM, HBM, VMEM],
        scratch_shapes=[
            pltpu.VMEM((rows, width), jnp.float32),
            pltpu.VMEM((rows, width), jnp.bfloat16),
            pltpu.SemaphoreType.DMA((2,)),
        ],
        compiler_params=pltpu.CompilerParams(vmem_limit_bytes=8 << 20),
        cost_estimate=pl.CostEstimate(
            flops=270_000_000, bytes_accessed=4_000_000, transcendentals=16
        ),
        name="dispatch",
    )(keep_a, got_a, keep_b, got_b, residual, gain, placing)


def turning(blocks, capacity, sources, back):
    lines = blocks * capacity * sources
    left = lax.broadcasted_iota(jnp.int32, (lines, lines), 0)
    right = lax.broadcasted_iota(jnp.int32, (lines, lines), 1)
    if back:
        left, right = right, left
    wanted = left % sources * (blocks * capacity) + left // sources
    return (wanted == right).astype(jnp.float32).astype(jnp.bfloat16)


def expert_kernel(
    arrived, gate, up, down, out_far, rows_in, hidden, rows_out, out_near, sems
):
    groups = rows_out.shape[0]
    width = rows_in.shape[1]
    sources = arrived.shape[0] // groups
    blocks = width // BLOCK
    lines = arrived.shape[1] * sources
    each = lines // blocks
    capacity = arrived.shape[1] // blocks
    turn = turning(blocks, capacity, sources, False)
    for g in range(groups):
        turned = jnp.dot(
            turn,
            arrived[g * sources : (g + 1) * sources].reshape(lines, BLOCK),
            preferred_element_type=jnp.float32,
        ).astype(jnp.bfloat16)
        for i in range(blocks):
            rows_in[g * each : (g + 1) * each, i * BLOCK : (i + 1) * BLOCK] = turned[
                i * each : (i + 1) * each
            ]
    units = hidden.shape[1]
    step = 256
    for at in range(0, units, step):
        lanes = slice(at, at + step)
        gated = jnp.dot(rows_in[...], gate[0, :, lanes], preferred_element_type=jnp.float32)
        raised = jnp.dot(rows_in[...], up[0, :, lanes], preferred_element_type=jnp.float32)
        hidden[:, lanes] = (gated / (1.0 + jnp.exp(-gated)) * raised).astype(jnp.bfloat16)
    for i in range(blocks):
        lanes = slice(i * BLOCK, (i + 1) * BLOCK)
        output = jnp.dot(hidden[...], down[0, :, lanes], preferred_element_type=jnp.float32)
        rows_out[:, i * each : (i + 1) * each, :] = output.astype(jnp.bfloat16).reshape(
            groups, each, BLOCK
        )
    turn = turning(blocks, capacity, sources, True)
    outward = []
    for g in range(groups):
        part = pl.ds(g * sources, sources)
        out_near[part] = (
            jnp.dot(turn, rows_out[g], preferred_element_type=jnp.float32)
            .astype(jnp.bfloat16)
            .reshape(sources, arrived.shape[1], BLOCK)
        )
        copy = pltpu.make_async_copy(out_near.at[part], out_far.at[part], sems.at[g])
        copy.start()
        outward.append(copy)
    for copy in outward:
        copy.wait()


def run_expert(arrived, gate, up, down):
    experts, lines, _ = arrived.shape
    _, width, units = gate.shape
    token_rows = experts * lines // (width // BLOCK)
    groups = token_rows // ROWS
    return pl.pallas_call(
        expert_kernel,
        out_shape=pltpu.HBM(arrived.shape, jnp.bfloat16),
        in_specs=[VMEM] * 4,
        out_specs=HBM,
        scratch_shapes=[
            pltpu.VMEM((token_rows, width), jnp.bfloat16),
            pltpu.VMEM((token_rows, units), jnp.bfloat16),
            pltpu.VMEM((groups, token_rows, BLOCK), jnp.bfloat16),
            pltpu.VMEM(arrived.shape, jnp.bfloat16),
            pltpu.SemaphoreType.DMA((groups,)),
        ],
        compiler_params=pltpu.CompilerParams(vmem_limit_bytes=12 << 20),
        cost_estimate=pl.CostEstimate(
            flops=5_900_000_000, bytes_accessed=23_000_000, transcendentals=200_000
        ),
        name="expert",
    )(
        arrived,
        *(pltpu.with_memory_space_constraint(array, pltpu.VMEM) for array in (gate, up, down)),
    )


def mixing_kernel(target_ref, gates, mixing_far, mixing_ref, sem):
    tall, wide = mixing_ref.shape
    target = target_ref[...].T
    gate_of = jnp.concatenate([gates[...]] * (tall // gates.shape[0]), axis=0)
    step = 256
    for at in range(0, wide, step):
        line = lax.broadcasted_iota(jnp.int32, (tall, step), 1) + at
        mixing = jnp.zeros((tall, step), jnp.float32)
        for k in range(target.shape[1]):
            mixing = jnp.where(line == target[:, k : k + 1], gate_of[:, k : k + 1], mixing)
        mixing_ref[:, at : at + step] = mixing.astype(jnp.bfloat16)
    copy = pltpu.make_async_copy(mixing_ref, mixing_far, sem)
    copy.start()
    copy.wait()


def mix(target, gates, lines):
    shape = (target.shape[1], lines)
    return pl.pallas_call(
        mixing_kernel,
        out_shape=pltpu.HBM(shape, jnp.bfloat16),
        in_specs=[VMEM, VMEM],
        out_specs=HBM,
        scratch_shapes=[pltpu.VMEM(shape, jnp.bfloat16), pltpu.SemaphoreType.DMA],
        compiler_params=pltpu.CompilerParams(vmem_limit_bytes=8 << 20),
        cost_estimate=pl.CostEstimate(flops=6_000_000, bytes_accessed=600_000, transcendentals=0),
        name="mixing",
    )(target, gates)


def combine_kernel(mixing_far, returned, hidden_far, out_ref, mixing, hidden, sems):
    rows = hidden.shape[0]
    copies = [
        pltpu.make_async_copy(mixing_far, mixing, sems.at[0]),
        pltpu.make_async_copy(hidden_far, hidden, sems.at[1]),
    ]
    for copy in copies:
        copy.start()
    copies[0].wait()
    mixed = jnp.dot(mixing[...], returned[...], preferred_element_type=jnp.float32)
    copies[1].wait()
    for i in range(mixed.shape[0] // rows):
        lanes = slice(i * BLOCK, (i + 1) * BLOCK)
        out_ref[:, lanes] = (hidden[:, lanes] + mixed[i * rows : (i + 1) * rows]).astype(
            jnp.bfloat16
        )


def combine(mixing, returned, hidden):
    far = [pltpu.with_memory_space_constraint(array, pltpu.HBM) for array in (mixing, hidden)]
    return pl.pallas_call(
        combine_kernel,
        out_shape=jax.ShapeDtypeStruct(hidden.shape, jnp.bfloat16),
        in_specs=[HBM, VMEM, HBM],
        out_specs=VMEM,
        scratch_shapes=[
            pltpu.VMEM(mixing.shape, jnp.bfloat16),
            pltpu.VMEM(hidden.shape, jnp.float32),
            pltpu.SemaphoreType.DMA((2,)),
        ],
        compiler_params=pltpu.CompilerParams(vmem_limit_bytes=8 << 20),
        cost_estimate=pl.CostEstimate(
            flops=270_000_000, bytes_accessed=3_000_000, transcendentals=0
        ),
        name="combine",
    )(far[0], returned, far[1])


def route_gates(logits, routes):
    matches = routes[:, :, None] == jnp.arange(logits.shape[1], dtype=jnp.int32)[None, None, :]
    chosen = jnp.sum(jnp.where(matches, logits[:, None, :], 0.0), axis=-1)
    raised = jnp.exp(chosen)
    return raised / jnp.sum(raised, axis=1, keepdims=True)


def add(left, right):
    return (left.astype(jnp.float32) + right.astype(jnp.float32)).astype(jnp.bfloat16)


def scatter_sum(regrouped, mine, beside, spot, peers):
    jump = {"y": 1, "Y": 3, "z": 4, "Z": 12}

    def swap(array, way):
        return lax.ppermute(array, "dev", [(i, i ^ (2 * jump[way])) for i in range(peers)])

    orders = ("yYzZ", "YyzZ", "zZyY", "ZzyY")
    masks = []
    for order in orders:
        places = []
        for place in range(16):
            mask = 0
            for bit, way in enumerate(order):
                if place >> (3 - bit) & 1:
                    mask ^= jump[way]
            places.append(mask)
        masks.append(tuple(places))
    sent = project(regrouped, mine, beside, spot, [places[8:] for places in masks], "project_sent")
    got = [swap(array, order[0]) for array, order in zip(sent, orders)]
    regrouped, _ = lax.optimization_barrier((regrouped, sent[0]))
    kept = list(
        project(regrouped, mine, beside, spot, [places[:8] for places in masks], "project_kept")
    )
    for part, order in enumerate(orders):
        both = add(kept[part], got[part])
        half = both.shape[0] // 2
        kept[part], got[part] = both[:half], swap(both[half:], order[1])
    merged = []
    for pair in (0, 2):
        way, last = orders[pair][2:]
        both = jnp.concatenate(
            [add(kept[pair], got[pair]), add(kept[pair + 1], got[pair + 1])], axis=2
        )
        merged.append((both[:2], swap(both[2:], way), last))
    ends = []
    for keep, arrived, last in merged:
        both = add(keep, arrived)
        ends += [both[0], swap(both[1], last)]
    return ends


def shards(
    queries,
    new_keys,
    new_values,
    key_pages,
    value_pages,
    block_tables,
    context_lengths,
    out_weight,
    residual,
    norm_gain,
    router_weight,
    routes,
    expert_gate,
    expert_up,
    expert_down,
):
    rows, width = residual.shape
    peers = lax.axis_size("dev")
    chips = peers // 2
    place = lax.axis_index("dev")
    spot = jnp.stack([place >> 1, place & 1])
    queries, spot = lax.optimization_barrier((queries, spot))
    same_core = [[2 * chip + side for chip in range(chips)] for side in range(2)]
    experts = router_weight.shape[1]
    blocks = width // BLOCK
    lines = blocks * CAPACITY

    attended, target = attend(
        queries,
        new_keys,
        new_values,
        key_pages,
        value_pages,
        block_tables,
        context_lengths,
        routes,
        chips,
        blocks,
    )
    attended, weight_sent = lax.optimization_barrier((attended, out_weight))
    weight_beside = lax.ppermute(weight_sent, "dev", [(i, i ^ 1) for i in range(peers)])
    regrouped = lax.all_to_all(
        attended, "dev", split_axis=0, concat_axis=0, axis_index_groups=same_core, tiled=True
    )
    ends = scatter_sum(regrouped, weight_sent, weight_beside, spot, peers)

    line = jnp.arange(experts * lines, dtype=jnp.int32)
    placed = line[:, None] == target[0][None, :]
    for k in range(1, target.shape[0]):
        placed = placed | (line[:, None] == target[k][None, :])
    placing = placed.astype(jnp.bfloat16)

    hidden_state, normed, sent = dispatch(*ends, residual, norm_gain[None], placing)
    arrived = lax.all_to_all(
        sent.reshape(experts, lines, BLOCK),
        ("attn", "dev"),
        split_axis=0,
        concat_axis=0,
        tiled=True,
    )
    output_rows = run_expert(arrived, expert_gate, expert_up, expert_down)
    returned = lax.all_to_all(
        output_rows, ("attn", "dev"), split_axis=0, concat_axis=0, tiled=True
    ).reshape(experts * lines, BLOCK)

    logits = jnp.dot(normed, router_weight, preferred_element_type=jnp.float32)
    gate_values = route_gates(logits, routes)
    mixing = mix(target, gate_values, experts * lines)
    return combine(mixing, returned, hidden_state)


def solution(mesh):
    in_specs = (
        P(("attn", "dev"), None),
        P(("attn", "dev"), None),
        P(("attn", "dev"), None),
        P(("attn", "dev"), None, None),
        P(("attn", "dev"), None, None),
        P(("attn", "dev"), None),
        P(("attn", "dev")),
        P("dev", None),
        P(("attn", "dev"), None),
        P(),
        P(),
        P(("attn", "dev"), None),
        P(("attn", "dev"), None, None),
        P(("attn", "dev"), None, None),
        P(("attn", "dev"), None, None),
    )
    out_specs = P(("attn", "dev"), None)
    return jax.shard_map(shards, mesh=mesh, in_specs=in_specs, out_specs=out_specs, check_vma=False)
```

```python
import functools
import math

import jax
import jax.numpy as jnp
from jax import lax
from jax.experimental import pallas as pl
from jax.experimental.pallas import tpu as pltpu
from jax.sharding import PartitionSpec as P

HEADS = 64
KVH = 4
HD = 128
GROUP = HEADS // KVH
MAXCTX = 64
PAGE = 16
EPSILON = 1e-06
BLOCK = 512
ROWS = 32
CAPACITY = 2
TOGETHER = 2
CONTRACT_LAST = (((1,), (1,)), ((), ()))
VMEM = pl.BlockSpec(memory_space=pltpu.VMEM)
SMEM = pl.BlockSpec(memory_space=pltpu.SMEM)
HBM = pl.BlockSpec(memory_space=pltpu.HBM)


def attention_kernel(
    tables_far,
    lengths_far,
    q_far,
    own_key_far,
    own_value_far,
    keys_far,
    values_far,
    routes_far,
    out_far,
    target_far,
    tables,
    lengths,
    routes,
    routes_near,
    target,
    q_near,
    own_key,
    own_value,
    keys,
    values,
    q_turned,
    out_turned,
    scores_held,
    own_held,
    weights_held,
    own_weights_held,
    out_near,
    sems,
    out_sems,
):
    rows = q_near.shape[0]
    pages = MAXCTX // PAGE
    tall, wide = TOGETHER * GROUP, TOGETHER * MAXCTX
    big = tall * KVH
    scale = 1.0 / math.sqrt(HD)
    inward = [
        pltpu.make_async_copy(far, near, sems.at[i])
        for i, (far, near) in enumerate(
            (
                (q_far, q_near),
                (own_key_far, own_key),
                (keys_far, keys),
                (values_far, values),
                (own_value_far, own_value),
                (tables_far, tables),
                (lengths_far, lengths),
                (routes_far, routes),
                (routes_far, routes_near),
            )
        )
    ]
    for copy in inward[:3] + inward[5:]:
        copy.start()
    inward[7].wait()
    inward[8].wait()
    chosen = routes_near[...]
    column = lax.broadcasted_iota(jnp.int32, chosen.shape, 1)
    rank = jnp.zeros_like(chosen)
    for t in range(rows - 1):
        named = jnp.zeros_like(chosen)
        for k in range(routes.shape[0]):
            named = jnp.where(chosen == routes[k, t], 1, named)
        rank = rank + jnp.where(column > t, named, 0)
    blocks = target.shape[1] // rows
    first_line = chosen * (blocks * CAPACITY) + rank
    target[...] = jnp.concatenate(
        [first_line + block * CAPACITY for block in range(blocks)], axis=1
    )
    target_copy = pltpu.make_async_copy(target, target_far, sems.at[9])
    target_copy.start()
    inward[0].wait()
    for head in range(HEADS):
        q_turned[head // GROUP, pl.ds(head % GROUP * rows, rows), :] = q_near[
            :, head * HD : (head + 1) * HD
        ].astype(jnp.float32)
    inward[1].wait()
    inward[2].wait()
    inward[3].start()
    inward[4].start()
    inward[5].wait()
    inward[6].wait()
    for first in range(0, rows, TOGETHER):
        page_ids = [tables[j, first + i] for i in range(TOGETHER) for j in range(pages)]
        for kv in range(KVH):
            lanes = slice(kv * HD, (kv + 1) * HD)
            q = jnp.concatenate(
                [
                    q_turned[kv, pl.ds(first + i, GROUP, stride=rows), :]
                    for i in range(TOGETHER)
                ],
                axis=0,
            ).astype(jnp.bfloat16)
            k = jnp.concatenate([keys[page, :, lanes] for page in page_ids], axis=0)
            at = pl.ds(first // TOGETHER * big + kv * tall, tall)
            scores_held[at, :] = (
                lax.dot_general(q, k, CONTRACT_LAST, preferred_element_type=jnp.float32) * scale
            )
            own_held[at, :] = (
                lax.dot_general(
                    q, own_key[:, lanes], CONTRACT_LAST, preferred_element_type=jnp.float32
                )
                * scale
            )
    row_request = lax.broadcasted_iota(jnp.int32, (big, wide), 0) // GROUP % TOGETHER
    place = lax.broadcasted_iota(jnp.int32, (big, wide), 1) - row_request * MAXCTX
    own_request = lax.broadcasted_iota(jnp.int32, (big, rows), 0) // GROUP % TOGETHER
    own_column = lax.broadcasted_iota(jnp.int32, (big, rows), 1)
    for first in range(0, rows, TOGETHER):
        at = pl.ds(first // TOGETHER * big, big)
        limit = jnp.zeros((big, wide), jnp.int32)
        for i in range(TOGETHER):
            limit = jnp.where(row_request == i, lengths[first + i], limit)
        scores = jnp.where((place >= 0) & (place < limit), scores_held[at, :], -jnp.inf)
        own_score = jnp.where(own_column == own_request + first, own_held[at, :], -jnp.inf)
        top = jnp.maximum(
            jnp.max(scores, axis=1, keepdims=True), jnp.max(own_score, axis=1, keepdims=True)
        )
        weights = jnp.exp(scores - top)
        own_weights = jnp.exp(own_score - top)
        share = 1.0 / (
            jnp.sum(weights, axis=1, keepdims=True) + jnp.sum(own_weights, axis=1, keepdims=True)
        )
        weights_held[at, :] = (weights * share).astype(jnp.bfloat16)
        own_weights_held[at, :] = (own_weights * share).astype(jnp.bfloat16)
    inward[3].wait()
    inward[4].wait()
    outward = []
    held = out_near.shape[2] // HD
    span = GROUP // held
    for kv in range(KVH):
        lanes = slice(kv * HD, (kv + 1) * HD)
        for first in range(0, rows, TOGETHER):
            page_ids = [tables[j, first + i] for i in range(TOGETHER) for j in range(pages)]
            at = pl.ds(first // TOGETHER * big + kv * tall, tall)
            v = jnp.concatenate([values[page, :, lanes] for page in page_ids], axis=0)
            blended = jnp.dot(
                weights_held[at, :], v, preferred_element_type=jnp.float32
            ) + jnp.dot(
                own_weights_held[at, :], own_value[:, lanes], preferred_element_type=jnp.float32
            )
            for i in range(TOGETHER):
                out_turned[kv, pl.ds(first + i, GROUP, stride=rows), :] = blended[
                    i * GROUP : (i + 1) * GROUP
                ]
        for head in range(kv * GROUP, (kv + 1) * GROUP):
            out_near[head // held, :, head % held * HD : (head % held + 1) * HD] = out_turned[
                kv, pl.ds(head % GROUP * rows, rows), :
            ].astype(jnp.bfloat16)
        part = pl.ds(kv * span, span)
        copy = pltpu.make_async_copy(out_near.at[part], out_far.at[part], out_sems.at[kv])
        copy.start()
        outward.append(copy)
    for copy in outward:
        copy.wait()
    target_copy.wait()


def attend(
    queries, new_keys, new_values, key_pool, value_pool, tables, lengths, routes, chips, blocks
):
    rows = queries.shape[0]
    total = HEADS * rows
    shape = (chips, rows, HEADS * HD // chips)
    wide = TOGETHER * MAXCTX
    bf16, f32 = jnp.bfloat16, jnp.float32
    return pl.pallas_call(
        attention_kernel,
        out_shape=[
            pltpu.HBM(shape, bf16),
            pltpu.HBM((routes.shape[1], blocks * rows), jnp.int32),
        ],
        in_specs=[HBM] * 8,
        out_specs=[HBM] * 2,
        scratch_shapes=[
            pltpu.SMEM(tables.shape[::-1], jnp.int32),
            pltpu.SMEM(lengths.shape, jnp.int32),
            pltpu.SMEM(routes.shape[::-1], jnp.int32),
            pltpu.VMEM(routes.shape[::-1], jnp.int32),
            pltpu.VMEM((routes.shape[1], blocks * rows), jnp.int32),
            pltpu.VMEM(queries.shape, bf16),
            pltpu.VMEM(new_keys.shape, bf16),
            pltpu.VMEM(new_values.shape, bf16),
            pltpu.VMEM(key_pool.shape, bf16),
            pltpu.VMEM(value_pool.shape, bf16),
            pltpu.VMEM((KVH, GROUP * rows, HD), f32),
            pltpu.VMEM((KVH, GROUP * rows, HD), f32),
            pltpu.VMEM((total, wide), f32),
            pltpu.VMEM((total, rows), f32),
            pltpu.VMEM((total, wide), bf16),
            pltpu.VMEM((total, rows), bf16),
            pltpu.VMEM(shape, bf16),
            pltpu.SemaphoreType.DMA((10,)),
            pltpu.SemaphoreType.DMA((KVH,)),
        ],
        compiler_params=pltpu.CompilerParams(vmem_limit_bytes=12 << 20),
        cost_estimate=pl.CostEstimate(
            flops=600_000_000, bytes_accessed=5_000_000, transcendentals=300_000
        ),
        name="attention",
    )(
        *(
            pltpu.with_memory_space_constraint(array, pltpu.HBM)
            for array in (
                tables.T,
                lengths,
                queries,
                new_keys,
                new_values,
                key_pool,
                value_pool,
                routes.T,
            )
        )
    )


def projection_kernel(orders, spot, x_ref, mine, beside, *outs):
    chip, core = spot[0], spot[1]
    depth = mine.shape[0]
    columns = outs[0].shape[2]
    for i, (masks, out) in enumerate(zip(orders, outs)):
        lanes = slice(i * columns, (i + 1) * columns)
        x = jnp.concatenate([x_ref[chip ^ mask] for mask in masks], axis=0)
        low, high = x[:, :depth], x[:, depth:]
        here = jnp.full(low.shape, core, jnp.int32) == 0
        out[...] = (
            (
                jnp.dot(
                    jnp.where(here, low, high),
                    mine[:, lanes],
                    preferred_element_type=jnp.float32,
                )
                + jnp.dot(
                    jnp.where(here, high, low),
                    beside[:, lanes],
                    preferred_element_type=jnp.float32,
                )
            )
            .astype(jnp.bfloat16)
            .reshape(out.shape)
        )


def project(regrouped, mine, beside, spot, orders, name):
    _, rows, _ = regrouped.shape
    columns = mine.shape[1] // len(orders)
    return pl.pallas_call(
        functools.partial(projection_kernel, orders),
        out_shape=[
            jax.ShapeDtypeStruct((len(masks), rows, columns), jnp.bfloat16) for masks in orders
        ],
        in_specs=[SMEM, VMEM, VMEM, VMEM],
        out_specs=[VMEM] * len(orders),
        compiler_params=pltpu.CompilerParams(vmem_limit_bytes=8 << 20),
        cost_estimate=pl.CostEstimate(
            flops=540_000_000, bytes_accessed=5_500_000, transcendentals=0
        ),
        name=name,
    )(
        spot,
        regrouped,
        pltpu.with_memory_space_constraint(mine, pltpu.VMEM),
        pltpu.with_memory_space_constraint(beside, pltpu.VMEM),
    )


def dispatch_kernel(
    keep_a,
    got_a,
    keep_b,
    got_b,
    residual,
    gain,
    placing,
    hidden_far,
    normed_far,
    sent_ref,
    hidden_ref,
    normed_ref,
    sems,
):
    rows = residual.shape[0]
    halves = []
    at = 0
    for keep, got in ((keep_a, got_a), (keep_b, got_b)):
        span = keep.shape[1]
        halves.append(
            residual[:, at : at + span].astype(jnp.float32)
            + (keep[...].astype(jnp.float32) + got[...].astype(jnp.float32))
        )
        at += span
    hidden = jnp.concatenate(halves, axis=1)
    hidden_ref[...] = hidden
    mean_square = jnp.mean(hidden * hidden, axis=1, keepdims=True)
    normed = (hidden * lax.rsqrt(mean_square + EPSILON) * gain[...]).astype(jnp.bfloat16)
    normed_ref[...] = normed
    copies = [
        pltpu.make_async_copy(hidden_ref, hidden_far, sems.at[0]),
        pltpu.make_async_copy(normed_ref, normed_far, sems.at[1]),
    ]
    for copy in copies:
        copy.start()
    blocks = at // BLOCK
    stacked = jnp.concatenate(
        [normed[:, i * BLOCK : (i + 1) * BLOCK] for i in range(blocks)], axis=0
    )
    step = 512
    for i in range(0, placing.shape[0], step):
        part = pl.ds(i, step)
        sent_ref[part, :] = jnp.dot(
            placing[part, :], stacked, preferred_element_type=jnp.float32
        ).astype(jnp.bfloat16)
    for copy in copies:
        copy.wait()


def dispatch(keep_a, got_a, keep_b, got_b, residual, gain, placing):
    rows, width = residual.shape
    return pl.pallas_call(
        dispatch_kernel,
        out_shape=[
            pltpu.HBM((rows, width), jnp.float32),
            pltpu.HBM((rows, width), jnp.bfloat16),
            jax.ShapeDtypeStruct((placing.shape[0], BLOCK), jnp.bfloat16),
        ],
        in_specs=[VMEM] * 7,
        out_specs=[HBM, HBM, VMEM],
        scratch_shapes=[
            pltpu.VMEM((rows, width), jnp.float32),
            pltpu.VMEM((rows, width), jnp.bfloat16),
            pltpu.SemaphoreType.DMA((2,)),
        ],
        compiler_params=pltpu.CompilerParams(vmem_limit_bytes=8 << 20),
        cost_estimate=pl.CostEstimate(
            flops=270_000_000, bytes_accessed=4_000_000, transcendentals=16
        ),
        name="dispatch",
    )(keep_a, got_a, keep_b, got_b, residual, gain, placing)


def turning(blocks, capacity, sources, back):
    lines = blocks * capacity * sources
    left = lax.broadcasted_iota(jnp.int32, (lines, lines), 0)
    right = lax.broadcasted_iota(jnp.int32, (lines, lines), 1)
    if back:
        left, right = right, left
    wanted = left % sources * (blocks * capacity) + left // sources
    return (wanted == right).astype(jnp.float32).astype(jnp.bfloat16)


def expert_kernel(
    arrived, gate, up, down, out_far, rows_in, hidden, rows_out, out_near, sems
):
    groups = rows_out.shape[0]
    width = rows_in.shape[1]
    sources = arrived.shape[0] // groups
    blocks = width // BLOCK
    lines = arrived.shape[1] * sources
    each = lines // blocks
    capacity = arrived.shape[1] // blocks
    turn = turning(blocks, capacity, sources, False)
    for g in range(groups):
        turned = jnp.dot(
            turn,
            arrived[g * sources : (g + 1) * sources].reshape(lines, BLOCK),
            preferred_element_type=jnp.float32,
        ).astype(jnp.bfloat16)
        for i in range(blocks):
            rows_in[g * each : (g + 1) * each, i * BLOCK : (i + 1) * BLOCK] = turned[
                i * each : (i + 1) * each
            ]
    units = hidden.shape[1]
    step = 256
    for at in range(0, units, step):
        lanes = slice(at, at + step)
        gated = jnp.dot(rows_in[...], gate[0, :, lanes], preferred_element_type=jnp.float32)
        raised = jnp.dot(rows_in[...], up[0, :, lanes], preferred_element_type=jnp.float32)
        hidden[:, lanes] = (gated / (1.0 + jnp.exp(-gated)) * raised).astype(jnp.bfloat16)
    for i in range(blocks):
        lanes = slice(i * BLOCK, (i + 1) * BLOCK)
        output = jnp.dot(hidden[...], down[0, :, lanes], preferred_element_type=jnp.float32)
        rows_out[:, i * each : (i + 1) * each, :] = output.astype(jnp.bfloat16).reshape(
            groups, each, BLOCK
        )
    turn = turning(blocks, capacity, sources, True)
    outward = []
    for g in range(groups):
        part = pl.ds(g * sources, sources)
        out_near[part] = (
            jnp.dot(turn, rows_out[g], preferred_element_type=jnp.float32)
            .astype(jnp.bfloat16)
            .reshape(sources, arrived.shape[1], BLOCK)
        )
        copy = pltpu.make_async_copy(out_near.at[part], out_far.at[part], sems.at[g])
        copy.start()
        outward.append(copy)
    for copy in outward:
        copy.wait()


def run_expert(arrived, gate, up, down):
    experts, lines, _ = arrived.shape
    _, width, units = gate.shape
    token_rows = experts * lines // (width // BLOCK)
    groups = token_rows // ROWS
    return pl.pallas_call(
        expert_kernel,
        out_shape=pltpu.HBM(arrived.shape, jnp.bfloat16),
        in_specs=[VMEM] * 4,
        out_specs=HBM,
        scratch_shapes=[
            pltpu.VMEM((token_rows, width), jnp.bfloat16),
            pltpu.VMEM((token_rows, units), jnp.bfloat16),
            pltpu.VMEM((groups, token_rows, BLOCK), jnp.bfloat16),
            pltpu.VMEM(arrived.shape, jnp.bfloat16),
            pltpu.SemaphoreType.DMA((groups,)),
        ],
        compiler_params=pltpu.CompilerParams(vmem_limit_bytes=12 << 20),
        cost_estimate=pl.CostEstimate(
            flops=5_900_000_000, bytes_accessed=23_000_000, transcendentals=200_000
        ),
        name="expert",
    )(
        arrived,
        *(pltpu.with_memory_space_constraint(array, pltpu.VMEM) for array in (gate, up, down)),
    )


def mixing_kernel(target_ref, gates, mixing_far, mixing_ref, sem):
    tall, wide = mixing_ref.shape
    target = target_ref[...].T
    gate_of = jnp.concatenate([gates[...]] * (tall // gates.shape[0]), axis=0)
    step = 256
    for at in range(0, wide, step):
        line = lax.broadcasted_iota(jnp.int32, (tall, step), 1) + at
        mixing = jnp.zeros((tall, step), jnp.float32)
        for k in range(target.shape[1]):
            mixing = jnp.where(line == target[:, k : k + 1], gate_of[:, k : k + 1], mixing)
        mixing_ref[:, at : at + step] = mixing.astype(jnp.bfloat16)
    copy = pltpu.make_async_copy(mixing_ref, mixing_far, sem)
    copy.start()
    copy.wait()


def mix(target, gates, lines):
    shape = (target.shape[1], lines)
    return pl.pallas_call(
        mixing_kernel,
        out_shape=pltpu.HBM(shape, jnp.bfloat16),
        in_specs=[VMEM, VMEM],
        out_specs=HBM,
        scratch_shapes=[pltpu.VMEM(shape, jnp.bfloat16), pltpu.SemaphoreType.DMA],
        compiler_params=pltpu.CompilerParams(vmem_limit_bytes=8 << 20),
        cost_estimate=pl.CostEstimate(flops=6_000_000, bytes_accessed=600_000, transcendentals=0),
        name="mixing",
    )(target, gates)


def combine_kernel(mixing_far, returned, hidden_far, out_ref, mixing, hidden, sems):
    rows = hidden.shape[0]
    copies = [
        pltpu.make_async_copy(mixing_far, mixing, sems.at[0]),
        pltpu.make_async_copy(hidden_far, hidden, sems.at[1]),
    ]
    for copy in copies:
        copy.start()
    copies[0].wait()
    mixed = jnp.dot(mixing[...], returned[...], preferred_element_type=jnp.float32)
    copies[1].wait()
    for i in range(mixed.shape[0] // rows):
        lanes = slice(i * BLOCK, (i + 1) * BLOCK)
        out_ref[:, lanes] = (hidden[:, lanes] + mixed[i * rows : (i + 1) * rows]).astype(
            jnp.bfloat16
        )


def combine(mixing, returned, hidden):
    far = [pltpu.with_memory_space_constraint(array, pltpu.HBM) for array in (mixing, hidden)]
    return pl.pallas_call(
        combine_kernel,
        out_shape=jax.ShapeDtypeStruct(hidden.shape, jnp.bfloat16),
        in_specs=[HBM, VMEM, HBM],
        out_specs=VMEM,
        scratch_shapes=[
            pltpu.VMEM(mixing.shape, jnp.bfloat16),
            pltpu.VMEM(hidden.shape, jnp.float32),
            pltpu.SemaphoreType.DMA((2,)),
        ],
        compiler_params=pltpu.CompilerParams(vmem_limit_bytes=8 << 20),
        cost_estimate=pl.CostEstimate(
            flops=270_000_000, bytes_accessed=3_000_000, transcendentals=0
        ),
        name="combine",
    )(far[0], returned, far[1])


def route_gates(logits, routes):
    matches = routes[:, :, None] == jnp.arange(logits.shape[1], dtype=jnp.int32)[None, None, :]
    chosen = jnp.sum(jnp.where(matches, logits[:, None, :], 0.0), axis=-1)
    raised = jnp.exp(chosen)
    return raised / jnp.sum(raised, axis=1, keepdims=True)


def add(left, right):
    return (left.astype(jnp.float32) + right.astype(jnp.float32)).astype(jnp.bfloat16)


def scatter_sum(regrouped, mine, beside, spot, peers):
    jump = {"y": 1, "Y": 3, "z": 4, "Z": 12}

    def swap(array, way):
        return lax.ppermute(array, "dev", [(i, i ^ (2 * jump[way])) for i in range(peers)])

    orders = ("yYzZ", "YyzZ", "zZyY", "ZzyY")
    masks = []
    for order in orders:
        places = []
        for place in range(16):
            mask = 0
            for bit, way in enumerate(order):
                if place >> (3 - bit) & 1:
                    mask ^= jump[way]
            places.append(mask)
        masks.append(tuple(places))
    sent = project(regrouped, mine, beside, spot, [places[8:] for places in masks], "project_sent")
    got = [swap(array, order[0]) for array, order in zip(sent, orders)]
    regrouped, _ = lax.optimization_barrier((regrouped, sent[0]))
    kept = list(
        project(regrouped, mine, beside, spot, [places[:8] for places in masks], "project_kept")
    )
    for part, order in enumerate(orders):
        both = add(kept[part], got[part])
        half = both.shape[0] // 2
        kept[part], got[part] = both[:half], swap(both[half:], order[1])
    merged = []
    for pair in (0, 2):
        way, last = orders[pair][2:]
        both = jnp.concatenate(
            [add(kept[pair], got[pair]), add(kept[pair + 1], got[pair + 1])], axis=2
        )
        merged.append((both[:2], swap(both[2:], way), last))
    ends = []
    for keep, arrived, last in merged:
        both = add(keep, arrived)
        ends += [both[0], swap(both[1], last)]
    return ends


def shards(
    queries,
    new_keys,
    new_values,
    key_pages,
    value_pages,
    block_tables,
    context_lengths,
    out_weight,
    residual,
    norm_gain,
    router_weight,
    routes,
    expert_gate,
    expert_up,
    expert_down,
):
    rows, width = residual.shape
    peers = lax.axis_size("dev")
    chips = peers // 2
    place = lax.axis_index("dev")
    spot = jnp.stack([place >> 1, place & 1])
    queries, spot = lax.optimization_barrier((queries, spot))
    same_core = [[2 * chip + side for chip in range(chips)] for side in range(2)]
    experts = router_weight.shape[1]
    blocks = width // BLOCK
    lines = blocks * CAPACITY

    attended, target = attend(
        queries,
        new_keys,
        new_values,
        key_pages,
        value_pages,
        block_tables,
        context_lengths,
        routes,
        chips,
        blocks,
    )
    attended, weight_sent = lax.optimization_barrier((attended, out_weight))
    weight_beside = lax.ppermute(weight_sent, "dev", [(i, i ^ 1) for i in range(peers)])
    regrouped = lax.all_to_all(
        attended, "dev", split_axis=0, concat_axis=0, axis_index_groups=same_core, tiled=True
    )
    ends = scatter_sum(regrouped, out_weight, weight_beside, spot, peers)

    line = jnp.arange(experts * lines, dtype=jnp.int32)
    placed = line[:, None] == target[0][None, :]
    for k in range(1, target.shape[0]):
        placed = placed | (line[:, None] == target[k][None, :])
    placing = placed.astype(jnp.bfloat16)

    hidden_state, normed, sent = dispatch(*ends, residual, norm_gain[None], placing)
    arrived = lax.all_to_all(
        sent.reshape(experts, lines, BLOCK),
        ("attn", "dev"),
        split_axis=0,
        concat_axis=0,
        tiled=True,
    )
    output_rows = run_expert(arrived, expert_gate, expert_up, expert_down)
    returned = lax.all_to_all(
        output_rows, ("attn", "dev"), split_axis=0, concat_axis=0, tiled=True
    ).reshape(experts * lines, BLOCK)

    logits = jnp.dot(normed, router_weight, preferred_element_type=jnp.float32)
    gate_values = route_gates(logits, routes)
    mixing = mix(target, gate_values, experts * lines)
    return combine(mixing, returned, hidden_state)


def solution(mesh):
    in_specs = (
        P(("attn", "dev"), None),
        P(("attn", "dev"), None),
        P(("attn", "dev"), None),
        P(("attn", "dev"), None, None),
        P(("attn", "dev"), None, None),
        P(("attn", "dev"), None),
        P(("attn", "dev")),
        P("dev", None),
        P(("attn", "dev"), None),
        P(),
        P(),
        P(("attn", "dev"), None),
        P(("attn", "dev"), None, None),
        P(("attn", "dev"), None, None),
        P(("attn", "dev"), None, None),
    )
    out_specs = P(("attn", "dev"), None)
    return jax.shard_map(shards, mesh=mesh, in_specs=in_specs, out_specs=out_specs, check_vma=False)
```
